128 devices in a mesh: dp: 8 (over y_hi, z), fsdp: 16 (over y_lo, x, core).
Axes of the slice: x: 4, y: 4 (y_hi: 2, y_lo: 2; y = y_hi * 2 + y_lo), z: 4, core: 2. Of those that a mesh axis runs over, the one named last changes fastest.
Arguments:
- hidden: bfloat16 [32768, 8192], P(('dp', 'fsdp')), may hold values from -6 to 6
- inner_raw: bfloat16 [32768, 8192], P(('dp', 'fsdp')), may hold values from -6 to 6
- gate_raw: bfloat16 [32768, 8192], P(('dp', 'fsdp')), may hold values from -6 to 6
- step_raw: float32 [32768, 128], P(('dp', 'fsdp')), may hold values from -6 to 6
- proj_weight: bfloat16 [8192, 2048], P('fsdp'), may hold values from -0.0625 to 0.0625
- conv_weight: float32 [4, 10240], replicated, may hold values from -3 to 3
- conv_bias: float32 [10240], replicated, may hold values from -0.5 to 0.5
- decay_log: float32 [128], replicated, may hold values from -9 to -3.5
- step_bias: float32 [128], replicated, may hold values from -1 to 1
- norm_gain: float32 [8192], replicated, may hold values from 0.5 to 1.5
- ssm_state: bfloat16 [16, 128, 64, 256], P('dp', 'fsdp'), may hold values from -96 to 96
- conv_state: bfloat16 [16, 3, 10240], P('dp'), may hold values from -6 to 6
- slot_prompt: int32 [128], P(('dp', 'fsdp')), may hold values from 0 to 15, as said below
- slot_len: int32 [128], P(('dp', 'fsdp')), may hold values from 32 to 256, as said below
Outputs:
- mixed: bfloat16 [32768, 8192], P(('dp', 'fsdp'))
The draws below stay inside these ranges and needn't reach their ends.
Inputs may be any that keep to these rules, and one draw needn't show every extreme that they name: `slot_prompt`: every prompt is continued by exactly 128 / 16 slots. `slot_len`: rows of a slot past its length are padding; some slot is full in every draw.
All inputs are finite; a program needn't handle non-finite values.
Results may differ from the reference program's by a relative error of at most 0.001.
Values may be sent and summed in bfloat16 or wider, within the bound.
A program may use at most 192 MiB of HBM per device.

```python
import jax
import jax.numpy as jnp
from jax import lax

D = 8192
HEADS = 128
P_SIZE = 64
N = 256
GROUPS = 4
K = 4
BLK = 128
LMAX = 256
PROMPTS = 16
SLOTS = 128
TOKENS = 32768
CH = 10240


def draw_slot_prompt(key, part):
    key = jax.random.fold_in(key, 11)
    order = jax.random.permutation(key, SLOTS)
    return (order // (SLOTS // PROMPTS)).astype(jnp.int32)


def draw_slot_len(key, part):
    key = jax.random.fold_in(key, 23)
    first_key, second_key = jax.random.split(key)
    lengths = jax.random.randint(first_key, (SLOTS,), LMAX // 8, LMAX + 1)
    full_slot = jax.random.randint(second_key, (), 0, SLOTS)
    return lengths.at[full_slot].set(LMAX).astype(jnp.int32)


def levels(stream_key, shape, shards, smallest, largest):
    level, own = 1.0, jax.random.fold_in(stream_key, 6)
    for position, shards_of in shards:
        heights = jnp.exp(jax.random.uniform(jax.random.fold_in(own, position), (shards_of,), jnp.float32, smallest / len(shards), largest / len(shards)))
        level = level * jnp.repeat(heights, shape[position] // shards_of).reshape([-1 if axis == position else 1 for axis in range(len(shape))])
    return level


def normal_values(own_key, extent, spread, most, cuts=(), kind=jnp.bfloat16):
    loudness = levels(own_key, extent, cuts, -0.22, 0.18) if cuts else 1.0
    result = jax.random.normal(own_key, extent, jnp.float32) * spread * loudness
    return jnp.minimum(jnp.maximum(result, -most), most).astype(kind)


def setup_inputs(seed: int = 0) -> dict:
    key_of = jax.random.split(jax.random.key(seed), 15)
    hidden = normal_values(key_of[0], (TOKENS, D), 1.0, 6.0, ((0, 128),))
    inner_raw = normal_values(key_of[1], (TOKENS, HEADS * P_SIZE), 1.0, 6.0, ((0, 128),))
    gate_raw = normal_values(key_of[2], (TOKENS, HEADS * P_SIZE), 1.0, 6.0, ((0, 128),))
    step_raw = normal_values(key_of[3], (TOKENS, HEADS), 1.0, 6.0, ((0, 128),), jnp.float32)
    proj_weight = normal_values(key_of[4], (D, 2 * GROUPS * N), D ** -0.5, 0.0625, ((0, 16),))
    conv_weight = normal_values(key_of[5], (K, CH), 0.5, 3.0, (), jnp.float32)
    conv_bias = jnp.clip(jax.random.uniform(key_of[6], (CH,), jnp.float32, -0.5, 0.5), -0.5, 0.5)
    decay_log = jnp.clip(jax.random.uniform(key_of[7], (HEADS,), jnp.float32, -9.0, -3.5), -9.0, -3.5)
    step_bias = jnp.clip(jax.random.uniform(key_of[8], (HEADS,), jnp.float32, -1.0, 1.0), -1.0, 1.0)
    norm_gain = jnp.clip(jax.random.uniform(key_of[9], (HEADS * P_SIZE,), jnp.float32, 0.5, 1.5), 0.5, 1.5)
    ssm_state = normal_values(key_of[10], (PROMPTS, HEADS, P_SIZE, N), 16.0, 96.0, ((0, 8), (1, 16)))
    conv_state = normal_values(key_of[11], (PROMPTS, K - 1, CH), 1.0, 6.0, ((0, 8),))
    slot_prompt = draw_slot_prompt(jax.random.fold_in(key_of[14], 71), 0)
    slot_len = draw_slot_len(jax.random.fold_in(key_of[14], 71), 0)
    return {"hidden": hidden, "inner_raw": inner_raw, "gate_raw": gate_raw, "step_raw": step_raw, "proj_weight": proj_weight, "conv_weight": conv_weight, "conv_bias": conv_bias, "decay_log": decay_log, "step_bias": step_bias, "norm_gain": norm_gain, "ssm_state": ssm_state, "conv_state": conv_state, "slot_prompt": slot_prompt, "slot_len": slot_len}


HIGHEST = lax.Precision.HIGHEST

def scan_blocks(inner_rows, b_rows, c_rows, step_sizes, decay_rate, start_state, block):
    row_count = inner_rows.shape[0]
    groups = start_state.shape[0]
    per_group = start_state.shape[1]
    head_dim = start_state.shape[2]
    state_dim = start_state.shape[3]
    blocks = row_count // block
    inner_blocks = inner_rows.reshape(blocks, block, groups, per_group, head_dim)
    b_blocks = b_rows.reshape(blocks, block, groups, state_dim)
    c_blocks = c_rows.reshape(blocks, block, groups, state_dim)
    step_blocks = step_sizes.reshape(blocks, block, groups, per_group)
    log_blocks = (step_sizes * decay_rate[None, :]).reshape(blocks, block, groups, per_group)
    places = jnp.arange(block)
    causal = places[:, None] >= places[None, :]

    def advance(carry_state, pieces):
        inner_piece, b_piece, c_piece, step_piece, log_piece = pieces
        summed = jnp.cumsum(log_piece, axis=0)
        scores = jnp.einsum('tgn,sgn->gts', c_piece, b_piece, precision=HIGHEST)
        moved = jnp.transpose(summed, (1, 2, 0))
        spread_log = moved[:, :, :, None] - moved[:, :, None, :]
        weights = jnp.exp(jnp.where(causal[None, None], spread_log, -jnp.inf))
        mixing = weights * scores[:, None] * jnp.transpose(step_piece, (1, 2, 0))[:, :, None, :]
        within = jnp.einsum('gkts,sgkp->tgkp', mixing, inner_piece, precision=HIGHEST)
        carried = jnp.einsum('tgn,gkpn->tgkp', c_piece, carry_state, precision=HIGHEST) * jnp.exp(summed)[:, :, :, None]
        to_end = jnp.exp(summed[-1][None] - summed) * step_piece
        added_state = jnp.einsum('sgk,sgkp,sgn->gkpn', to_end, inner_piece, b_piece, precision=HIGHEST)
        carry_state = jnp.exp(summed[-1])[:, :, None, None] * carry_state + added_state
        return (carry_state, within + carried)
    final_state, outputs = lax.scan(advance, start_state, (inner_blocks, b_blocks, c_blocks, step_blocks, log_blocks))
    return outputs.reshape(row_count, groups * per_group * head_dim)

def mixer(projected, inner_raw, gate_raw, step_raw, conv_weight, conv_bias, decay_log, step_bias, norm_gain, start_state, conv_rows, length, block):
    channels = jnp.concatenate([inner_raw.astype(jnp.float32), projected], axis=1)
    padded = jnp.concatenate([conv_rows.astype(jnp.float32), channels], axis=0)
    kernel_size = conv_weight.shape[0]
    row_count = channels.shape[0]
    convolved = jnp.zeros_like(channels) + conv_bias[None, :]
    for offset in range(kernel_size):
        convolved = convolved + conv_weight[offset][None, :] * padded[offset:offset + row_count]
    activated = jax.nn.silu(convolved)
    features = inner_raw.shape[1]
    state_cols = (channels.shape[1] - features) // 2
    heads = step_raw.shape[1]
    state_dim = start_state.shape[2]
    groups = state_cols // state_dim
    inner_rows = activated[:, :features]
    b_rows = activated[:, features:features + state_cols]
    c_rows = activated[:, features + state_cols:]
    step_sizes = jax.nn.softplus(step_raw + step_bias[None, :])
    decay_rate = -jnp.exp(decay_log)
    grouped_state = start_state.astype(jnp.float32).reshape(groups, heads // groups, start_state.shape[1], state_dim)
    output = scan_blocks(inner_rows, b_rows, c_rows, step_sizes, decay_rate, grouped_state, block)
    gated_out = output * jax.nn.silu(gate_raw.astype(jnp.float32))
    grouped = gated_out.reshape(row_count, groups, features // groups)
    scale_rows = lax.rsqrt(lax.optimization_barrier(jnp.mean(grouped * grouped, axis=2, keepdims=True)) + 1e-05)
    normed = (grouped * scale_rows).reshape(row_count, features) * norm_gain[None, :]
    live_rows = jnp.arange(row_count) < length
    return jnp.where(live_rows[:, None], normed, 0.0).astype(jnp.bfloat16)

def reference(hidden, inner_raw, gate_raw, step_raw, proj_weight, conv_weight, conv_bias, decay_log, step_bias, norm_gain, ssm_state, conv_state, slot_prompt, slot_len):

    def one_slot(slot_index):
        first_row = (slot_index * LMAX).astype(jnp.int32)

        def slice_rows(array):
            return lax.dynamic_slice_in_dim(array, first_row, LMAX, 0)
        prompt = lax.dynamic_index_in_dim(slot_prompt, slot_index, 0, keepdims=False)
        length = lax.dynamic_index_in_dim(slot_len, slot_index, 0, keepdims=False)
        projected = jnp.dot(slice_rows(hidden), proj_weight, preferred_element_type=jnp.float32)
        start_state = lax.dynamic_index_in_dim(ssm_state, prompt, 0, keepdims=False)
        conv_rows = lax.dynamic_index_in_dim(conv_state, prompt, 0, keepdims=False)
        return mixer(projected, slice_rows(inner_raw), slice_rows(gate_raw), slice_rows(step_raw), conv_weight, conv_bias, decay_log, step_bias, norm_gain, start_state, conv_rows, length, BLK)
    results = lax.map(one_slot, jnp.arange(SLOTS, dtype=jnp.int32))
    return results.reshape(SLOTS * LMAX, HEADS * P_SIZE)
```

```python
import jax
import jax.numpy as jnp
from jax import lax
from jax.experimental import pallas as pl
from jax.experimental.pallas import tpu as pltpu
from jax.sharding import PartitionSpec as P

F32 = jnp.float32
BF16 = jnp.bfloat16
PIECE = 512


def split_two(value):
    high = value.astype(BF16)
    return high, (value - high.astype(F32)).astype(BF16)


def dot_nn(left, right):
    return jnp.dot(left, right, preferred_element_type=F32)


def dot_nt(left, right):
    return lax.dot_general(left, right, (((1,), (1,)), ((), ())), preferred_element_type=F32)


def silu(value):
    half = 0.5 * value
    return half + half * jnp.tanh(half)


def convolve(pad_ref, rows, first, taps, bias):
    count = rows.shape[0]
    pad_ref[5:8, :] = first
    pad_ref[8 : 8 + count, :] = rows
    total = taps[3:4, :] * rows + bias
    for k in range(3):
        total = total + taps[k : k + 1, :] * pad_ref[5 + k : 5 + k + count, :]
    return total


def before_kernel(
    inner_ref, gate_ref, step_ref, decay_ref, step_bias_ref, taps_ref, bias_ref, first_ref,
    high_ref, low_ref, gate_out_ref,
    pad_ref, heads_ref, grow_ref, fall_ref,
):
    tile = pl.program_id(0)
    count = inner_ref.shape[0]
    width = inner_ref.shape[1]
    heads = step_ref.shape[1]

    @pl.when(tile == 0)
    def _():
        raw = step_ref[...] + step_bias_ref[...]
        steps = jnp.maximum(raw, 0.0) + jnp.log1p(jnp.exp(-jnp.abs(raw)))
        logs = -jnp.exp(decay_ref[...]) * steps
        place = lax.broadcasted_iota(jnp.int32, (count, count), 0)
        other = lax.broadcasted_iota(jnp.int32, (count, count), 1)
        lower = jnp.where(place >= other, 1.0, 0.0).astype(BF16)
        top = logs.astype(BF16)
        rest = logs - top.astype(F32)
        mid, last = split_two(rest)
        summed = dot_nn(lower, top) + (dot_nn(lower, mid) + dot_nn(lower, last))
        grow_ref[:, :heads], grow_ref[:, heads:] = split_two(steps * jnp.exp(-summed))
        fall_ref[:, :heads], fall_ref[:, heads:] = split_two(jnp.exp(summed))
        head = lax.broadcasted_iota(jnp.int32, (2 * heads, width), 0)
        column = lax.broadcasted_iota(jnp.int32, (2 * heads, width), 1)
        heads_ref[...] = jnp.where(head >= heads, head - heads, head) - column // 64

    spread = jnp.where(heads_ref[...] == tile * (width // 64), 1.0, 0.0).astype(BF16)
    rows = inner_ref[...].astype(F32)
    active = silu(convolve(pad_ref, rows, first_ref[...].astype(F32), taps_ref[...], bias_ref[...]))
    high_ref[...], low_ref[...] = split_two(active * dot_nn(grow_ref[...], spread))
    gate_out_ref[...] = silu(gate_ref[...].astype(F32)) * dot_nn(fall_ref[...], spread)


def before(inner_raw, gate_raw, step_raw, decay_log, step_bias, conv_weight, conv_bias, conv_rows):
    count, features = inner_raw.shape
    heads = step_raw.shape[1]
    width = PIECE
    across = lambda rows: pl.BlockSpec((rows, width), lambda j: (0, j))
    whole = lambda rows: pl.BlockSpec((rows, heads), lambda j: (0, 0))
    return pl.pallas_call(
        before_kernel,
        grid=(features // width,),
        in_specs=[
            across(count), across(count), whole(count), whole(1), whole(1),
            across(4), across(1), across(3),
        ],
        out_specs=[across(count), across(count), across(count)],
        out_shape=[
            jax.ShapeDtypeStruct((count, features), BF16),
            jax.ShapeDtypeStruct((count, features), BF16),
            jax.ShapeDtypeStruct((count, features), F32),
        ],
        scratch_shapes=[
            pltpu.VMEM((count + 8, width), F32),
            pltpu.VMEM((2 * heads, width), jnp.int32),
            pltpu.VMEM((count, 2 * heads), BF16),
            pltpu.VMEM((count, 2 * heads), BF16),
        ],
        compiler_params=pltpu.CompilerParams(vmem_limit_bytes=32 * 2**20),
        name="before_scan",
    )(inner_raw, gate_raw, step_raw, decay_log, step_bias, conv_weight, conv_bias, conv_rows)


def after_kernel(
    length_ref, b_ref, c_ref, b_taps_ref, c_taps_ref, b_bias_ref, c_bias_ref, b_first_ref, c_first_ref,
    state_ref, high_ref, low_ref, gate_ref, gain_ref, out_ref, pad_ref, gated_ref,
):
    count = b_ref.shape[0]
    features = high_ref.shape[1]

    def channel(rows, first, taps, bias):
        return split_two(
            silu(convolve(pad_ref, rows[...], first[...].astype(F32), taps[...], bias[...]))
        )

    b_high, b_low = channel(b_ref, b_first_ref, b_taps_ref, b_bias_ref)
    c_high, c_low = channel(c_ref, c_first_ref, c_taps_ref, c_bias_ref)
    scores = dot_nt(c_high, b_high) + (dot_nt(c_high, b_low) + dot_nt(c_low, b_high))
    place = lax.broadcasted_iota(jnp.int32, (count, count), 0)
    other = lax.broadcasted_iota(jnp.int32, (count, count), 1)
    m_high, m_low = split_two(jnp.where(place >= other, scores, 0.0))
    squares = jnp.zeros((count, 128), F32)
    for low in range(0, features, PIECE):
        cols = slice(low, low + PIECE)
        state = state_ref[cols, :]
        total = dot_nt(c_high, state) + dot_nt(c_low, state)
        total = total + dot_nn(m_high, high_ref[:, cols])
        total = total + (dot_nn(m_high, low_ref[:, cols]) + dot_nn(m_low, high_ref[:, cols]))
        gated = total * gate_ref[:, cols]
        gated_ref[:, cols] = gated
        for at in range(0, PIECE, 128):
            part = gated[:, at : at + 128]
            squares = squares + part * part
    mean = jnp.sum(squares, axis=1, keepdims=True) * (1.0 / features)
    row = lax.broadcasted_iota(jnp.int32, (count, 1), 0)
    scale = jnp.where(row < length_ref[0], lax.rsqrt(mean + 1e-05), 0.0)
    for low in range(0, features, PIECE):
        cols = slice(low, low + PIECE)
        out_ref[:, cols] = (gated_ref[:, cols] * scale * gain_ref[:, cols]).astype(BF16)


def after(length, projected, conv_weight, conv_bias, conv_rows, state, high, low, gate, norm_gain):
    count, features = high.shape
    n = state.shape[1]
    groups = projected.shape[1] // (2 * n)
    width = features // groups
    first_b = features // n
    at = lambda rows, base: pl.BlockSpec((rows, n), lambda g, base=base: (0, base + g))
    wide = lambda rows: pl.BlockSpec((rows, width), lambda g: (0, g))
    return pl.pallas_call(
        after_kernel,
        grid=(groups,),
        in_specs=[
            pl.BlockSpec(memory_space=pltpu.SMEM),
            at(count, 0), at(count, groups),
            at(4, first_b), at(4, first_b + groups),
            at(1, first_b), at(1, first_b + groups),
            at(3, first_b), at(3, first_b + groups),
            pl.BlockSpec((width, n), lambda g: (g, 0)),
            wide(count), wide(count), wide(count), wide(1),
        ],
        out_specs=wide(count),
        out_shape=jax.ShapeDtypeStruct((count, features), BF16),
        scratch_shapes=[pltpu.VMEM((count + 8, n), F32), pltpu.VMEM((count, width), F32)],
        compiler_params=pltpu.CompilerParams(vmem_limit_bytes=40 * 2**20),
        name="scan_and_norm",
    )(
        length, projected, projected, conv_weight, conv_weight, conv_bias, conv_bias,
        conv_rows, conv_rows, state, high, low, gate, norm_gain,
    )


def on_device(
    hidden, inner_raw, gate_raw, step_raw, proj_weight, conv_weight, conv_bias, decay_log, step_bias,
    norm_gain, ssm_state, conv_state, slot_prompt, slot_len,
):
    prompt = slot_prompt[0]
    conv_bias = conv_bias[None, :]
    conv_all = lax.all_gather(conv_state, "dp", axis=0, tiled=True)
    conv_rows = lax.dynamic_index_in_dim(conv_all, prompt, 0, keepdims=False)
    states = lax.all_gather(ssm_state, "dp", axis=0, tiled=True)
    owners = lax.all_gather(slot_prompt, "fsdp", axis=0, tiled=True)
    high, low, gate = before(
        inner_raw, gate_raw, step_raw, decay_log[None, :], step_bias[None, :],
        conv_weight, conv_bias, conv_rows,
    )
    projected = jnp.dot(
        hidden,
        lax.all_gather(proj_weight, "fsdp", axis=0, tiled=True),
        preferred_element_type=F32,
    )
    outgoing = jnp.take(states, owners, axis=0)
    arrived = lax.all_to_all(outgoing, "fsdp", split_axis=0, concat_axis=0, tiled=True)
    state = arrived.reshape(-1, arrived.shape[3])
    return after(
        slot_len, projected, conv_weight, conv_bias, conv_rows, state, high, low, gate,
        norm_gain[None, :],
    )


def solution(mesh):
    rows = P(("dp", "fsdp"), None)
    in_specs = (
        rows, rows, rows, rows, P("fsdp", None), P(), P(), P(), P(), P(),
        P("dp", "fsdp", None, None), P("dp", None, None), P(("dp", "fsdp")), P(("dp", "fsdp")),
    )
    return jax.shard_map(on_device, mesh=mesh, in_specs=in_specs, out_specs=rows, check_vma=False)
```

```python
import jax
import jax.numpy as jnp
from jax import lax
from jax.experimental import pallas as pl
from jax.experimental.pallas import tpu as pltpu
from jax.sharding import PartitionSpec as P

F32 = jnp.float32
BF16 = jnp.bfloat16
PIECE = 512
HEAD_ROWS = 16


def split_two(value):
    high = value.astype(BF16)
    return high, (value - high.astype(F32)).astype(BF16)


def dot_nn(left, right):
    return jnp.dot(left, right, preferred_element_type=F32)


def dot_nt(left, right):
    return lax.dot_general(left, right, (((1,), (1,)), ((), ())), preferred_element_type=F32)


def silu(value):
    half = 0.5 * value
    return half + half * jnp.tanh(half)


def convolve(pad_ref, rows, first, taps, bias):
    count = rows.shape[0]
    pad_ref[5:8, :] = first
    pad_ref[8 : 8 + count, :] = rows
    total = taps[3:4, :] * rows + bias
    for k in range(3):
        total = total + taps[k : k + 1, :] * pad_ref[5 + k : 5 + k + count, :]
    return total


def before_kernel(
    inner_ref, gate_ref, step_ref, decay_ref, step_bias_ref, taps_ref, bias_ref,
    high_ref, low_ref, gate_out_ref, factor_ref,
    pad_ref, heads_ref, grow_ref, fall_ref,
):
    tile = pl.program_id(0)
    count = inner_ref.shape[0]
    width = inner_ref.shape[1]
    heads = step_ref.shape[1]

    @pl.when(tile == 0)
    def _():
        raw = step_ref[...] + step_bias_ref[...]
        steps = jnp.maximum(raw, 0.0) + jnp.log1p(jnp.exp(-jnp.abs(raw)))
        logs = -jnp.exp(decay_ref[...]) * steps
        place = lax.broadcasted_iota(jnp.int32, (count, count), 0)
        other = lax.broadcasted_iota(jnp.int32, (count, count), 1)
        lower = jnp.where(place >= other, 1.0, 0.0).astype(BF16)
        top = logs.astype(BF16)
        rest = logs - top.astype(F32)
        mid, last = split_two(rest)
        summed = dot_nn(lower, top) + (dot_nn(lower, mid) + dot_nn(lower, last))
        grow_ref[:, :heads], grow_ref[:, heads:] = split_two(steps * jnp.exp(-summed))
        fall_ref[:, :heads], fall_ref[:, heads:] = split_two(jnp.exp(summed))
        head = lax.broadcasted_iota(jnp.int32, (2 * heads, width), 0)
        column = lax.broadcasted_iota(jnp.int32, (2 * heads, width), 1)
        heads_ref[...] = jnp.where(head >= heads, head - heads, head) - column // 64

    spread = jnp.where(heads_ref[...] == tile * (width // 64), 1.0, 0.0).astype(BF16)
    rows = inner_ref[...].astype(F32)
    factor = dot_nn(grow_ref[...], spread)
    factor_ref[...] = factor[:HEAD_ROWS, :]
    none = jnp.zeros((3, width), F32)
    active = silu(convolve(pad_ref, rows, none, taps_ref[...], bias_ref[...]))
    high_ref[...], low_ref[...] = split_two(active * factor)
    gate_out_ref[...] = silu(gate_ref[...].astype(F32)) * dot_nn(fall_ref[...], spread)


def before(inner_raw, gate_raw, step_raw, decay_log, step_bias, conv_weight, conv_bias):
    count, features = inner_raw.shape
    heads = step_raw.shape[1]
    width = PIECE
    across = lambda rows: pl.BlockSpec((rows, width), lambda j: (0, j))
    whole = lambda rows: pl.BlockSpec((rows, heads), lambda j: (0, 0))
    return pl.pallas_call(
        before_kernel,
        grid=(features // width,),
        in_specs=[
            across(count), across(count), whole(count), whole(1), whole(1),
            across(4), across(1),
        ],
        out_specs=[across(count), across(count), across(count), across(HEAD_ROWS)],
        out_shape=[
            jax.ShapeDtypeStruct((count, features), BF16),
            jax.ShapeDtypeStruct((count, features), BF16),
            jax.ShapeDtypeStruct((count, features), F32),
            jax.ShapeDtypeStruct((HEAD_ROWS, features), F32),
        ],
        scratch_shapes=[
            pltpu.VMEM((count + 8, width), F32),
            pltpu.VMEM((2 * heads, width), jnp.int32),
            pltpu.VMEM((count, 2 * heads), BF16),
            pltpu.VMEM((count, 2 * heads), BF16),
        ],
        compiler_params=pltpu.CompilerParams(vmem_limit_bytes=32 * 2**20),
        name="before_scan",
    )(inner_raw, gate_raw, step_raw, decay_log, step_bias, conv_weight, conv_bias)


def after_kernel(
    length_ref, b_ref, c_ref, b_taps_ref, c_taps_ref, taps_ref, b_bias_ref, c_bias_ref, bias_ref,
    b_first_ref, c_first_ref, first_ref, state_ref, inner_ref, factor_ref,
    high_ref, low_ref, gate_ref, gain_ref, out_ref, pad_ref, head_pad_ref, gated_ref,
):
    count = b_ref.shape[0]
    features = high_ref.shape[1]

    def channel(pad, rows, first, taps, bias):
        return silu(convolve(pad, rows[...].astype(F32), first[...].astype(F32), taps[...], bias[...]))

    head_rows = channel(head_pad_ref, inner_ref, first_ref, taps_ref, bias_ref) * factor_ref[...]
    head_high, head_low = split_two(head_rows)
    b_high, b_low = split_two(channel(pad_ref, b_ref, b_first_ref, b_taps_ref, b_bias_ref))
    c_high, c_low = split_two(channel(pad_ref, c_ref, c_first_ref, c_taps_ref, c_bias_ref))
    scores = dot_nt(c_high, b_high) + (dot_nt(c_high, b_low) + dot_nt(c_low, b_high))
    place = lax.broadcasted_iota(jnp.int32, (count, count), 0)
    other = lax.broadcasted_iota(jnp.int32, (count, count), 1)
    m_high, m_low = split_two(jnp.where(place >= other, scores, 0.0))
    squares = jnp.zeros((count, 128), F32)
    for low in range(0, features, PIECE):
        cols = slice(low, low + PIECE)
        state = state_ref[low // PIECE]
        high = jnp.concatenate([head_high[:, cols], high_ref[HEAD_ROWS:, cols]], axis=0)
        rest = jnp.concatenate([head_low[:, cols], low_ref[HEAD_ROWS:, cols]], axis=0)
        total = dot_nt(c_high, state) + dot_nt(c_low, state)
        total = total + dot_nn(m_high, high)
        total = total + (dot_nn(m_high, rest) + dot_nn(m_low, high))
        gated = total * gate_ref[:, cols]
        gated_ref[:, cols] = gated
        for at in range(0, PIECE, 128):
            part = gated[:, at : at + 128]
            squares = squares + part * part
    mean = jnp.sum(squares, axis=1, keepdims=True) * (1.0 / features)
    row = lax.broadcasted_iota(jnp.int32, (count, 1), 0)
    scale = jnp.where(row < length_ref[0], lax.rsqrt(mean + 1e-05), 0.0)
    for low in range(0, features, PIECE):
        cols = slice(low, low + PIECE)
        out_ref[:, cols] = (gated_ref[:, cols] * scale * gain_ref[:, cols]).astype(BF16)


def after(
    length, projected, conv_weight, conv_bias, conv_rows, state, inner_raw, factor, high, low, gate, norm_gain
):
    count, features = high.shape
    n = state.shape[2]
    groups = projected.shape[1] // (2 * n)
    width = features // groups
    first_b = features // n
    at = lambda rows, base: pl.BlockSpec((rows, n), lambda g, base=base: (0, base + g))
    wide = lambda rows: pl.BlockSpec((rows, width), lambda g: (0, g))
    return pl.pallas_call(
        after_kernel,
        grid=(groups,),
        in_specs=[
            pl.BlockSpec(memory_space=pltpu.SMEM),
            at(count, 0), at(count, groups),
            at(4, first_b), at(4, first_b + groups), wide(4),
            at(1, first_b), at(1, first_b + groups), wide(1),
            at(3, first_b), at(3, first_b + groups), wide(3),
            pl.BlockSpec((width // PIECE, PIECE, n), lambda g: (g, 0, 0)),
            wide(HEAD_ROWS), wide(HEAD_ROWS),
            wide(count), wide(count), wide(count), wide(1),
        ],
        out_specs=wide(count),
        out_shape=jax.ShapeDtypeStruct((count, features), BF16),
        scratch_shapes=[
            pltpu.VMEM((count + 8, n), F32),
            pltpu.VMEM((HEAD_ROWS + 8, width), F32),
            pltpu.VMEM((count, width), F32),
        ],
        compiler_params=pltpu.CompilerParams(vmem_limit_bytes=40 * 2**20),
        name="scan_and_norm",
    )(
        length, projected, projected, conv_weight, conv_weight, conv_weight, conv_bias, conv_bias, conv_bias,
        conv_rows, conv_rows, conv_rows, state, inner_raw, factor, high, low, gate, norm_gain,
    )


EXTRA = 16
QUARTER = 512
MESH = pl.DeviceIdType.MESH


def exchange_kernel(
    prompt_ref, hidden_ref, weight_ref, states_ref, projected_ref, arrived_ref,
    weights, rows, states, outgoing, prompts, prompt_words, partial, total, landed,
    w_send, w_recv, z_send, z_recv, d_send, d_recv, s_send, s_recv, o_send, o_recv,
    p_send, p_recv, h_send, h_recv, t_send, t_recv, local_sem,
):
    dp, fsdp = lax.axis_index("dp"), lax.axis_index("fsdp")
    z, x, core = dp % 4, (fsdp // 2) % 4, fsdp % 2
    y = (dp // 4) * 2 + fsdp // 8
    parity = y % 2
    half_cols = 4096
    count = hidden_ref.shape[0]

    def device(xx, yy, zz, cc):
        xx, yy, zz, cc = xx % 4, yy % 4, zz % 4, cc % 2
        return ((yy // 2) * 4 + zz, ((yy % 2) * 4 + xx) * 2 + cc)

    sibling = device(x, y, z, core + 1)
    x_up, x_down = device(x + 1, y, z, core), device(x + 3, y, z, core)
    z_up, z_down = device(x, y, z + 1, core), device(x, y, z + 3, core)
    across = device(x, y + 2, z, core)
    partner = device(x, y + 1 + 2 * core, z, core + 1)

    def remote(src, dst, send, recv, to):
        return pltpu.make_async_remote_copy(
            src_ref=src, dst_ref=dst, send_sem=send, recv_sem=recv, device_id=to, device_id_type=MESH
        )

    sent = []

    def send(src, dst, send_sem, recv_sem, to):
        copy = remote(src, dst, send_sem, recv_sem, to)
        copy.start()
        sent.append(copy)

    def landing(dst, recv_sem):
        remote(dst, dst, recv_sem, recv_sem, sibling).wait_recv()

    barrier = pltpu.get_barrier_semaphore()

    def greet(to):
        pl.semaphore_signal(barrier, inc=1, device_id=to, device_id_type=MESH)

    for dx in range(4):
        for dc in range(2):
            if dx or dc:
                greet(device(x + dx, y, z, core + dc))
            greet(device(x + dx, y + 1, z, core + dc))
            greet(device(x + dx, y + 3, z, core + dc))
    for to in (z_up, z_down, across):
        greet(to)
    pl.semaphore_wait(barrier, 26)

    me = x * 2 + core
    prompts[0, me] = jnp.full((8, 128), prompt_ref[0], jnp.int32)
    mine = prompts.at[0, me]

    def tell(i, _):
        dx, dc = i // 2, i % 2

        @pl.when(i > 0)
        def _():
            remote(mine, prompts.at[0, me], p_send.at[0, i], p_recv.at[0, me], device(x + dx, y, z, core + dc)).start()

        remote(mine, prompts.at[2, me], p_send.at[1, i], p_recv.at[2, me], device(x + dx, y + 1, z, core + dc)).start()
        remote(mine, prompts.at[1, me], p_send.at[2, i], p_recv.at[1, me], device(x + dx, y + 3, z, core + dc)).start()
        return 0

    lax.fori_loop(0, 8, tell, 0)

    def unit(of):
        return states.at[pl.ds(2 * of, 2)]

    def dp_at(yy, zz):
        return ((yy % 4) // 2) * 4 + zz % 4

    unit_here, unit_across = dp_at(y, z), dp_at(y + 2, z)
    keep_states = pltpu.make_async_copy(states_ref, unit(unit_here), local_sem.at[0])
    keep_states.start()
    send(states_ref, unit(unit_here), s_send.at[0], s_recv.at[0], across)
    send(states_ref, unit(unit_here), s_send.at[1], s_recv.at[1], z_up)
    send(states_ref, unit(unit_here), s_send.at[2], s_recv.at[2], z_down)

    def block(xx, cc):
        return ((xx % 4) * 2 + cc % 2) * 512

    def weight_at(quarter, xx, cc, low=0, many=512):
        return weights.at[quarter % 4, pl.ds(pl.multiple_of(block(xx, cc) + low, 256), many)]

    def own_quarter(quarter):
        return weight_ref.at[:, pl.ds(pl.multiple_of((quarter % 4) * QUARTER, QUARTER), QUARTER)]

    send(own_quarter(z), weight_at(z, x, core), w_send.at[0], w_recv.at[0], x_up)
    send(own_quarter(z), weight_at(z, x, core), w_send.at[1], w_recv.at[1], x_down)
    theirs = pl.ds(pl.multiple_of((1 - parity) * half_cols, half_cols), half_cols)
    ours = pl.ds(pl.multiple_of(parity * half_cols, half_cols), half_cols)
    send(hidden_ref.at[:, theirs], rows.at[pl.ds(0, count)], h_send.at[0], h_recv.at[0], partner)
    keep_rows = pltpu.make_async_copy(hidden_ref.at[:, ours], rows.at[pl.ds(count, count)], local_sem.at[1])
    keep_rows.start()
    keep_weights = []
    for step in range(4):
        at = (0, 1, 3, 2)[step]
        send(own_quarter(z + at), weight_at(z + at, x, core), d_send.at[at], d_recv.at[at], sibling)
        copy = pltpu.make_async_copy(own_quarter(z + at), weight_at(z + at, x, core), local_sem.at[2 + at])
        copy.start()
        keep_weights.append(copy)

    def pass_on(quarter_step, dx, slot):
        whole = weight_at(z + quarter_step, x + dx, core)
        send(whole, whole, d_send.at[slot], d_recv.at[slot], sibling)

    def along_z(dx):
        whole = weight_at(z, x + dx, core)
        at = (3, 1, 2).index(dx)
        send(whole, whole, z_send.at[at], z_recv.at[at], z_up)
        send(whole, whole, z_send.at[3 + at], z_recv.at[3 + at], z_down)

    landing(unit(unit_across), s_recv.at[0])
    send(unit(unit_across), unit(unit_across), s_send.at[3], s_recv.at[3], z_up)
    send(unit(unit_across), unit(unit_across), s_send.at[4], s_recv.at[4], z_down)

    landing(weight_at(z, x + 3, core), w_recv.at[0])
    first = weight_at(z, x + 3, core, 0, 256)
    send(first, first, w_send.at[2], w_recv.at[2], x_up)
    along_z(3)
    pass_on(0, 3, 4)
    landing(weight_at(z, x + 1, core), w_recv.at[1])
    second = weight_at(z, x + 1, core, 256, 256)
    send(second, second, w_send.at[3], w_recv.at[3], x_down)
    along_z(1)
    pass_on(0, 1, 5)

    def state_hop(yy, base, up_slot, down_slot, send_slot):
        below, above = dp_at(yy, z + 3), dp_at(yy, z + 1)
        landing(unit(below), s_recv.at[up_slot])
        one = states.at[2 * below]
        send(one, one, s_send.at[send_slot], s_recv.at[send_slot], z_up)
        landing(unit(above), s_recv.at[down_slot])
        other = states.at[2 * above + 1]
        send(other, other, s_send.at[send_slot + 1], s_recv.at[send_slot + 1], z_down)

    state_hop(y, 0, 1, 2, 5)
    landing(weight_at(z, x + 2, core, 0, 256), w_recv.at[2])
    landing(weight_at(z, x + 2, core, 256, 256), w_recv.at[3])
    along_z(2)
    pass_on(0, 2, 6)
    state_hop(y + 2, 0, 3, 4, 7)

    def multiply(step, slots):
        quarter = (z + step) % 4
        keep_weights[(0, 1, 3, 2).index(step)].wait()
        landing(weight_at(quarter, x, core + 1), d_recv.at[step])
        for dx, slot in zip((3, 1, 2), slots):
            landing(weight_at(quarter, x + dx, core + 1), d_recv.at[slot])

        def columns(n, _):
            cols = pl.ds(pl.multiple_of(n * 256, 256), 256)
            partial[step, :, cols] = dot_nn(rows[:count, :], weights[quarter, :, cols])
            return 0

        lax.fori_loop(0, 2, columns, 0)
        send(partial.at[step], landed.at[step], t_send.at[step], t_recv.at[step], partner)

        def own_columns(n, _):
            cols = pl.ds(pl.multiple_of(n * 256, 256), 256)
            total[step, :, cols] = dot_nn(rows[count:, :], weights[quarter, :, cols])
            return 0

        lax.fori_loop(0, 2, own_columns, 0)

    landing(rows.at[pl.ds(0, count)], h_recv.at[0])
    keep_rows.wait()
    multiply(0, (4, 5, 6))

    keep_states.wait()
    for yy, slot in ((y, 5), (y + 2, 7)):
        far = dp_at(yy, z + 2)
        landing(states.at[2 * far], s_recv.at[slot])
        landing(states.at[2 * far + 1], s_recv.at[slot + 1])

    def heard(i, _):
        @pl.when(i != me)
        def _():
            landing(prompts.at[0, i], p_recv.at[0, i])

        landing(prompts.at[1, i], p_recv.at[1, i])
        landing(prompts.at[2, i], p_recv.at[2, i])
        return 0

    lax.fori_loop(0, 8, heard, 0)
    words = pltpu.make_async_copy(prompts, prompt_words, local_sem.at[6])
    words.start()
    words.wait()
    lows = (0, 0, 256)
    many = (PIECE + EXTRA, 256, 256 + EXTRA)

    def give(i, _):
        dx, dc = i // 2, i % 2
        to_x, to_core = (x + dx) % 4, (core + dc) % 2
        at = to_x * 2 + to_core
        for kind in range(3):
            low, size = lows[kind], many[kind]
            outgoing[i, kind, pl.ds(0, size)] = states[prompt_words[kind, at, 0, 0], pl.ds(low, size)]
            src = outgoing.at[i, kind, pl.ds(0, size)]
            dst = arrived_ref.at[fsdp, pl.ds(low, size)]
            to = device(to_x, y + (0, 1, 3)[kind], z, to_core)
            if kind == 0:
                @pl.when(i > 0)
                def _():
                    remote(src, dst, o_send.at[kind, i], o_recv.at[kind, me], to).start()

                @pl.when(i == 0)
                def _():
                    pltpu.make_async_copy(src, dst, local_sem.at[7]).start()
            else:
                remote(src, dst, o_send.at[kind, i], o_recv.at[kind, me], to).start()
        return 0

    lax.fori_loop(0, 8, give, 0)

    for dx, at in ((3, 0), (1, 1), (2, 2)):
        below = weight_at(z + 3, x + dx, core)
        landing(below, z_recv.at[at])
        one = weight_at(z + 3, x + dx, core, 0, 256)
        send(one, one, z_send.at[6 + at], z_recv.at[6 + at], z_up)
        pass_on(3, dx, 7 + at)
        above = weight_at(z + 1, x + dx, core)
        landing(above, z_recv.at[3 + at])
        other = weight_at(z + 1, x + dx, core, 256, 256)
        send(other, other, z_send.at[9 + at], z_recv.at[9 + at], z_down)
        pass_on(1, dx, 10 + at)
    multiply(1, (10, 11, 12))
    multiply(3, (7, 8, 9))
    for dx, at in ((3, 0), (1, 1), (2, 2)):
        landing(weight_at(z + 2, x + dx, core, 0, 256), z_recv.at[6 + at])
        landing(weight_at(z + 2, x + dx, core, 256, 256), z_recv.at[9 + at])
        pass_on(2, dx, 13 + at)
    multiply(2, (13, 14, 15))

    for step in (0, 1, 3, 2):
        landing(landed.at[step], t_recv.at[step])
        cols = pl.ds(pl.multiple_of(((z + step) % 4) * QUARTER, QUARTER), QUARTER)
        projected_ref[:, cols] = total[step] + landed[step]

    def settle(i, _):
        @pl.when(i != me)
        def _():
            landing(arrived_ref.at[parity * 8 + i], o_recv.at[0, i])

        other = (1 - parity) * 8 + i
        landing(arrived_ref.at[other, pl.ds(0, many[1])], o_recv.at[1, i])
        landing(arrived_ref.at[other, pl.ds(lows[2], many[2])], o_recv.at[2, i])

        @pl.when(i > 0)
        def _():
            remote(mine, mine, p_send.at[0, i], p_recv.at[0, i], sibling).wait_send()
            remote(outgoing.at[i, 0], outgoing.at[i, 0], o_send.at[0, i], o_recv.at[0, i], sibling).wait_send()

        for kind in (1, 2):
            src = outgoing.at[i, kind, pl.ds(0, many[kind])]
            remote(mine, mine, p_send.at[kind, i], p_recv.at[kind, i], sibling).wait_send()
            remote(src, src, o_send.at[kind, i], o_recv.at[kind, i], sibling).wait_send()
        return 0

    lax.fori_loop(0, 8, settle, 0)
    pltpu.make_async_copy(outgoing.at[0, 0], arrived_ref.at[fsdp], local_sem.at[7]).wait()
    for copy in sent:
        copy.wait_send()


def exchange(hidden, weight, states, prompt):
    count = hidden.shape[0]
    columns = weight.shape[1]
    deep = PIECE + EXTRA
    dma = lambda *shape: pltpu.SemaphoreType.DMA(shape)
    anywhere = pl.BlockSpec(memory_space=pl.ANY)
    return pl.pallas_call(
        exchange_kernel,
        in_specs=[pl.BlockSpec(memory_space=pltpu.SMEM), anywhere, anywhere, anywhere],
        out_specs=[pl.BlockSpec(memory_space=pltpu.VMEM), anywhere],
        out_shape=[
            jax.ShapeDtypeStruct((count, columns), F32),
            jax.ShapeDtypeStruct((16, deep, 256), BF16),
        ],
        scratch_shapes=[
            pltpu.VMEM((4, 4096, QUARTER), BF16),
            pltpu.VMEM((2 * count, 4096), BF16),
            pltpu.VMEM((16, deep, 256), BF16),
            pltpu.VMEM((8, 3, deep, 256), BF16),
            pltpu.VMEM((3, 8, 8, 128), jnp.int32),
            pltpu.SMEM((3, 8, 8, 128), jnp.int32),
            pltpu.VMEM((4, count, QUARTER), F32),
            pltpu.VMEM((4, count, QUARTER), F32),
            pltpu.VMEM((4, count, QUARTER), F32),
            dma(4), dma(4), dma(12), dma(12), dma(16), dma(16), dma(9), dma(9), dma(3, 8), dma(3, 8),
            dma(3, 8), dma(3, 8), dma(1), dma(1), dma(4), dma(4), dma(8),
        ],
        compiler_params=pltpu.CompilerParams(
            collective_id=0, has_side_effects=True, vmem_limit_bytes=56 * 2**20
        ),
        cost_estimate=pl.CostEstimate(flops=9 * 10**9, bytes_accessed=2**25, transcendentals=0),
        name="exchange",
    )(prompt, hidden, weight, states)


def on_device(
    hidden, inner_raw, gate_raw, step_raw, proj_weight, conv_weight, conv_bias, decay_log, step_bias,
    norm_gain, ssm_state, conv_state, slot_prompt, slot_len,
):
    conv_bias = conv_bias[None, :]
    part = lax.axis_index("fsdp")
    share = conv_state.shape[2] // 16
    prompts = conv_state.shape[0]
    piece = lax.dynamic_slice_in_dim(conv_state, part * share, share, axis=2).reshape(prompts, 3 * share)
    piece = jnp.pad(piece, ((0, 0), (0, EXTRA * 256 - 3 * share))).reshape(prompts, EXTRA, 256)
    own_states = jnp.concatenate([ssm_state.reshape(prompts, PIECE, 256), piece], axis=1)
    projected, state = exchange(hidden, proj_weight, own_states, slot_prompt)
    conv_rows = state[:, PIECE:, :].reshape(16, EXTRA * 256)[:, : 3 * share].reshape(16, 3, share)
    conv_rows = conv_rows.transpose(1, 0, 2).reshape(3, 16 * share)
    high, low, gate, factor = before(
        inner_raw, gate_raw, step_raw, decay_log[None, :], step_bias[None, :], conv_weight, conv_bias
    )
    return after(
        slot_len, projected, conv_weight, conv_bias, conv_rows, state, inner_raw, factor, high, low, gate,
        norm_gain[None, :],
    )


def solution(mesh):
    rows = P(("dp", "fsdp"), None)
    in_specs = (
        rows, rows, rows, rows, P("fsdp", None), P(), P(), P(), P(), P(),
        P("dp", "fsdp", None, None), P("dp", None, None), P(("dp", "fsdp")), P(("dp", "fsdp")),
    )
    return jax.shard_map(on_device, mesh=mesh, in_specs=in_specs, out_specs=rows, check_vma=False)
```

```python
import jax
import jax.numpy as jnp
from jax import lax
from jax.experimental import pallas as pl
from jax.experimental.pallas import tpu as pltpu
from jax.sharding import PartitionSpec as P

F32 = jnp.float32
BF16 = jnp.bfloat16
PIECE = 512
HEAD_ROWS = 16


def split_two(value):
    high = value.astype(BF16)
    return high, (value - high.astype(F32)).astype(BF16)


def dot_nn(left, right):
    return jnp.dot(left, right, preferred_element_type=F32)


def dot_nt(left, right):
    return lax.dot_general(left, right, (((1,), (1,)), ((), ())), preferred_element_type=F32)


def silu(value):
    half = 0.5 * value
    return half + half * jnp.tanh(half)


def convolve(pad_ref, rows, first, taps, bias):
    count = rows.shape[0]
    pad_ref[5:8, :] = first
    pad_ref[8 : 8 + count, :] = rows
    total = taps[3:4, :] * rows + bias
    for k in range(3):
        total = total + taps[k : k + 1, :] * pad_ref[5 + k : 5 + k + count, :]
    return total


def after_kernel(
    length_ref, b_ref, c_ref, b_taps_ref, c_taps_ref, taps_ref, b_bias_ref, c_bias_ref, bias_ref,
    b_first_ref, c_first_ref, first_ref, state_ref, inner_ref, factor_ref,
    high_ref, low_ref, gate_ref, gain_ref, out_ref, pad_ref, head_pad_ref, gated_ref,
):
    count = b_ref.shape[0]
    features = high_ref.shape[1]

    def channel(pad, rows, first, taps, bias):
        return silu(convolve(pad, rows[...].astype(F32), first[...].astype(F32), taps[...], bias[...]))

    head_rows = channel(head_pad_ref, inner_ref, first_ref, taps_ref, bias_ref) * factor_ref[...]
    head_high, head_low = split_two(head_rows)
    b_high, b_low = split_two(channel(pad_ref, b_ref, b_first_ref, b_taps_ref, b_bias_ref))
    c_high, c_low = split_two(channel(pad_ref, c_ref, c_first_ref, c_taps_ref, c_bias_ref))
    scores = dot_nt(c_high, b_high) + (dot_nt(c_high, b_low) + dot_nt(c_low, b_high))
    place = lax.broadcasted_iota(jnp.int32, (count, count), 0)
    other = lax.broadcasted_iota(jnp.int32, (count, count), 1)
    m_high, m_low = split_two(jnp.where(place >= other, scores, 0.0))
    squares = jnp.zeros((count, 128), F32)
    for low in range(0, features, PIECE):
        cols = slice(low, low + PIECE)
        state = state_ref[low // PIECE]
        high = jnp.concatenate([head_high[:, cols], high_ref[HEAD_ROWS:, cols]], axis=0)
        rest = jnp.concatenate([head_low[:, cols], low_ref[HEAD_ROWS:, cols]], axis=0)
        total = dot_nt(c_high, state) + dot_nt(c_low, state)
        total = total + dot_nn(m_high, high)
        total = total + (dot_nn(m_high, rest) + dot_nn(m_low, high))
        gated = total * gate_ref[:, cols]
        gated_ref[:, cols] = gated
        for at in range(0, PIECE, 128):
            part = gated[:, at : at + 128]
            squares = squares + part * part
    mean = jnp.sum(squares, axis=1, keepdims=True) * (1.0 / features)
    row = lax.broadcasted_iota(jnp.int32, (count, 1), 0)
    scale = jnp.where(row < length_ref[0], lax.rsqrt(mean + 1e-05), 0.0)
    for low in range(0, features, PIECE):
        cols = slice(low, low + PIECE)
        out_ref[:, cols] = (gated_ref[:, cols] * scale * gain_ref[:, cols]).astype(BF16)


def after(
    length, projected, conv_weight, conv_bias, conv_rows, state, inner_raw, factor, high, low, gate, norm_gain
):
    count, features = high.shape
    n = state.shape[2]
    groups = projected.shape[1] // (2 * n)
    width = features // groups
    first_b = features // n
    at = lambda rows, base: pl.BlockSpec((rows, n), lambda g, base=base: (0, base + g))
    wide = lambda rows: pl.BlockSpec((rows, width), lambda g: (0, g))
    return pl.pallas_call(
        after_kernel,
        grid=(groups,),
        in_specs=[
            pl.BlockSpec(memory_space=pltpu.SMEM),
            at(count, 0), at(count, groups),
            at(4, first_b), at(4, first_b + groups), wide(4),
            at(1, first_b), at(1, first_b + groups), wide(1),
            at(3, first_b), at(3, first_b + groups), wide(3),
            pl.BlockSpec((width // PIECE, PIECE, n), lambda g: (g, 0, 0)),
            wide(HEAD_ROWS), wide(HEAD_ROWS),
            wide(count), wide(count), wide(count), wide(1),
        ],
        out_specs=wide(count),
        out_shape=jax.ShapeDtypeStruct((count, features), BF16),
        scratch_shapes=[
            pltpu.VMEM((count + 8, n), F32),
            pltpu.VMEM((HEAD_ROWS + 8, width), F32),
            pltpu.VMEM((count, width), F32),
        ],
        compiler_params=pltpu.CompilerParams(vmem_limit_bytes=62 * 2**20),
        name="scan_and_norm",
    )(
        length, projected, projected, conv_weight, conv_weight, conv_weight, conv_bias, conv_bias, conv_bias,
        conv_rows, conv_rows, conv_rows, state, inner_raw, factor, high, low, gate, norm_gain,
    )


EXTRA = 16
DIRECT = 512
SHARED = 384
MESH = pl.DeviceIdType.MESH
FAR = (3, 1, 2)
HALVES = ((0, 256), (256, 256 + EXTRA))
SPANS = (HALVES, ((0, 128), (256, 128)), ((128, 128), (384, 128 + EXTRA)))


def exchange_kernel(
    prompt_ref, hidden_ref, weight_ref, states_ref, inner_ref, gate_ref, step_ref, decay_ref,
    step_bias_ref, taps_ref, bias_ref,
    projected_ref, arrived_ref, high_ref, low_ref, gate_out_ref, factor_ref,
    shared, direct, rows, states_a, states_b, outgoing, prompts, prompt_words, partial, total, landed,
    partial_d, total_d, landed_d, inner, gate, gate_out, pad_ref, heads_ref, grow_ref, fall_ref,
    w_send, w_recv, x_send, x_recv, z_send, z_recv, d_send, d_recv, s_send, s_recv, o_send, o_recv,
    p_send, p_recv, h_send, h_recv, t_send, t_recv, local_sem,
):
    dp, fsdp = lax.axis_index("dp"), lax.axis_index("fsdp")
    z, x, core = dp % 4, (fsdp // 2) % 4, fsdp % 2
    y = (dp // 4) * 2 + fsdp // 8
    parity = y % 2
    depth = rows.shape[1]
    count = hidden_ref.shape[0]

    def device(xx, yy, zz, cc):
        xx, yy, zz, cc = xx % 4, yy % 4, zz % 4, cc % 2
        return ((yy // 2) * 4 + zz, ((yy % 2) * 4 + xx) * 2 + cc)

    sibling = device(x, y, z, core + 1)
    x_up, x_down = device(x + 1, y, z, core), device(x + 3, y, z, core)
    z_up, z_down = device(x, y, z + 1, core), device(x, y, z + 3, core)
    across = device(x, y + 2, z, core)
    partner = device(x, y + 1 + 2 * core, z, core + 1)

    def remote(src, dst, send, recv, to):
        return pltpu.make_async_remote_copy(
            src_ref=src, dst_ref=dst, send_sem=send, recv_sem=recv, device_id=to, device_id_type=MESH
        )

    sent = []

    def send(src, dst, send_sem, recv_sem, to):
        copy = remote(src, dst, send_sem, recv_sem, to)
        copy.start()
        sent.append(copy)

    def landing(dst, recv_sem):
        remote(dst, dst, recv_sem, recv_sem, sibling).wait_recv()

    def local(src, dst, at):
        copy = pltpu.make_async_copy(src, dst, local_sem.at[at])
        copy.start()
        return copy

    barrier = pltpu.get_barrier_semaphore()

    def greet(to):
        pl.semaphore_signal(barrier, inc=1, device_id=to, device_id_type=MESH)

    for dx in range(4):
        for dc in range(2):
            if dx or dc:
                greet(device(x + dx, y, z, core + dc))
            greet(device(x + dx, y + 1, z, core + dc))
            greet(device(x + dx, y + 3, z, core + dc))
    for to in (z_up, z_down, across):
        greet(to)
    keep_inner = local(inner_ref, inner, 0)
    keep_gate = local(gate_ref, gate, 1)
    me = x * 2 + core
    prompts[0, me] = jnp.full((8, 128), prompt_ref[0], jnp.int32)
    mine = prompts.at[0, me]
    pl.semaphore_wait(barrier, 26)

    states = (states_a, states_b)

    def unit(of, half):
        return states[half].at[pl.ds(2 * of, 2)]

    def one(of, which, half):
        return states[half].at[2 * of + which]

    def dp_at(yy, zz):
        return ((yy % 4) // 2) * 4 + zz % 4

    unit_here, unit_across = dp_at(y, z), dp_at(y + 2, z)

    def own_states(half, slot, to):
        src = states_ref.at[:, pl.ds(*HALVES[half])]
        send(src, unit(unit_here, half), s_send.at[half, slot], s_recv.at[half, slot], to)

    def own_along(half):
        own_states(half, 1, z_up)
        own_states(half, 2, z_down)

    def across_along(half):
        there = unit(unit_across, half)
        landing(there, s_recv.at[half, 0])
        send(there, there, s_send.at[half, 3], s_recv.at[half, 3], z_up)
        send(there, there, s_send.at[half, 4], s_recv.at[half, 4], z_down)

    def hop(half, yy, slot, onward):
        below, above = dp_at(yy, z + 3), dp_at(yy, z + 1)
        landing(unit(below, half), s_recv.at[half, slot])
        first = one(below, 0, half)
        send(first, first, s_send.at[half, onward], s_recv.at[half, onward], z_up)
        landing(unit(above, half), s_recv.at[half, slot + 1])
        second = one(above, 1, half)
        send(second, second, s_send.at[half, onward + 1], s_recv.at[half, onward + 1], z_down)

    def far_states(half):
        for yy, slot in ((y, 5), (y + 2, 7)):
            far = dp_at(yy, z + 2)
            landing(one(far, 0, half), s_recv.at[half, slot])
            landing(one(far, 1, half), s_recv.at[half, slot + 1])

    def block(xx, cc, low):
        return pl.multiple_of(((xx % 4) * 2 + cc % 2) * 512 + low, 256)

    def shared_at(step, xx, cc, low=0, many=512):
        return shared.at[(z + step) % 4, pl.ds(block(xx, cc, low), many)]

    def direct_at(xx, cc, low=0, many=512):
        return direct.at[pl.ds(block(xx, cc, low), many)]

    def own_shared(step):
        low = DIRECT + ((z + step) % 4) * SHARED
        return weight_ref.at[:, pl.ds(pl.multiple_of(low, 128), SHARED)]

    own_direct = weight_ref.at[:, pl.ds(0, DIRECT)]

    def to_sibling(ref, slot):
        send(ref, ref, d_send.at[slot], d_recv.at[slot], sibling)

    def along_z(at):
        whole = shared_at(0, x + FAR[at], core)
        send(whole, whole, z_send.at[at], z_recv.at[at], z_up)
        send(whole, whole, z_send.at[3 + at], z_recv.at[3 + at], z_down)

    def tell(i, _):
        dx, dc = i // 2, i % 2

        @pl.when(i > 0)
        def _():
            remote(mine, mine, p_send.at[0, i], p_recv.at[0, me], device(x + dx, y, z, core + dc)).start()

        remote(mine, prompts.at[2, me], p_send.at[1, i], p_recv.at[2, me], device(x + dx, y + 1, z, core + dc)).start()
        remote(mine, prompts.at[1, me], p_send.at[2, i], p_recv.at[1, me], device(x + dx, y + 3, z, core + dc)).start()
        return 0

    own_states(0, 0, across)
    own_along(0)
    send(own_shared(0), shared_at(0, x, core), w_send.at[0], w_recv.at[0], x_up)
    send(own_shared(0), shared_at(0, x, core), w_send.at[1], w_recv.at[1], x_down)
    lax.fori_loop(0, 8, tell, 0)
    keep_states = [
        local(states_ref.at[:, pl.ds(*HALVES[half])], unit(unit_here, half), (2, 15)[half]) for half in range(2)
    ]
    theirs = pl.ds(pl.multiple_of((1 - parity) * depth, depth), depth)
    ours = pl.ds(pl.multiple_of(parity * depth, depth), depth)
    keep_rows = local(hidden_ref.at[:, ours], rows.at[pl.ds(count, count)], 3)
    keep = {}
    for step in (0, 1, 3, 2):
        send(own_shared(step), shared_at(step, x, core), d_send.at[step], d_recv.at[step], sibling)
        keep[step] = local(own_shared(step), shared_at(step, x, core), 4 + step)
    send(own_direct, direct_at(x, core), d_send.at[4], d_recv.at[4], sibling)
    keep_direct = local(own_direct, direct_at(x, core), 8)

    heads = step_ref.shape[1]

    def decays():
        raw = step_ref[...] + step_bias_ref[...]
        steps = jnp.maximum(raw, 0.0) + jnp.log1p(jnp.exp(-jnp.abs(raw)))
        logs = -jnp.exp(decay_ref[...]) * steps
        place = lax.broadcasted_iota(jnp.int32, (count, count), 0)
        other = lax.broadcasted_iota(jnp.int32, (count, count), 1)
        lower = jnp.where(place >= other, 1.0, 0.0).astype(BF16)
        top = logs.astype(BF16)
        mid, last = split_two(logs - top.astype(F32))
        summed = dot_nn(lower, top) + (dot_nn(lower, mid) + dot_nn(lower, last))
        grow_ref[:, :heads], grow_ref[:, heads:] = split_two(steps * jnp.exp(-summed))
        fall_ref[:, :heads], fall_ref[:, heads:] = split_two(jnp.exp(summed))
        head = lax.broadcasted_iota(jnp.int32, (2 * heads, PIECE), 0)
        column = lax.broadcasted_iota(jnp.int32, (2 * heads, PIECE), 1)
        heads_ref[...] = jnp.where(head >= heads, head - heads, head) - column // 64

    def prepare(tile, _):
        cols = pl.ds(pl.multiple_of(tile * PIECE, PIECE), PIECE)
        spread = jnp.where(heads_ref[...] == tile * (PIECE // 64), 1.0, 0.0).astype(BF16)
        factor = dot_nn(grow_ref[...], spread)
        factor_ref[:, cols] = factor[:HEAD_ROWS, :]
        none = jnp.zeros((3, PIECE), F32)
        active = silu(convolve(pad_ref, inner[:, cols].astype(F32), none, taps_ref[:, cols], bias_ref[:, cols]))
        gate_out[:, cols] = silu(gate[:, cols].astype(F32)) * dot_nn(fall_ref[...], spread)
        inner[:, cols], gate[:, cols] = split_two(active * factor)
        return 0

    keep_inner.wait()
    keep_gate.wait()
    decays()
    lax.fori_loop(0, 3, prepare, 0)

    across_along(0)
    own_states(1, 0, across)
    hop(0, y, 1, 5)
    landing(shared_at(0, x + 3, core), w_recv.at[0])
    first = shared_at(0, x + 3, core, 0, 256)
    send(first, first, w_send.at[2], w_recv.at[2], x_up)
    to_sibling(shared_at(0, x + 3, core), 5)
    landing(shared_at(0, x + 1, core), w_recv.at[1])
    second = shared_at(0, x + 1, core, 256, 256)
    send(second, second, w_send.at[3], w_recv.at[3], x_down)
    to_sibling(shared_at(0, x + 1, core), 6)
    send(own_direct, direct_at(x, core), x_send.at[0], x_recv.at[0], x_up)
    send(own_direct, direct_at(x, core), x_send.at[1], x_recv.at[1], x_down)
    hop(0, y + 2, 3, 7)
    own_along(1)
    across_along(1)
    send(hidden_ref.at[:, theirs], rows.at[pl.ds(0, count)], h_send.at[0], h_recv.at[0], partner)

    def heard(i, _):
        @pl.when(i != me)
        def _():
            landing(prompts.at[0, i], p_recv.at[0, i])

        landing(prompts.at[1, i], p_recv.at[1, i])
        landing(prompts.at[2, i], p_recv.at[2, i])
        return 0

    def give(half):
        def step(i, _):
            to_x, to_core = (x + i // 2) % 4, (core + i % 2) % 2
            at = to_x * 2 + to_core
            for kind in range(3):
                low, size = SPANS[kind][half]
                span = pl.ds(low, size)
                outgoing[min(kind, 1), i, span] = states[half][
                    prompt_words[kind, at, 0, 0], pl.ds(low - HALVES[half][0], size)
                ]
                src = outgoing.at[min(kind, 1), i, span]
                dst = arrived_ref.at[fsdp, span]
                copy = remote(
                    src, dst, o_send.at[half, kind, i], o_recv.at[half, kind, me],
                    device(to_x, y + (0, 1, 3)[kind], z, to_core),
                )
                if kind == 0:
                    pl.when(i > 0)(copy.start)

                    @pl.when(i == 0)
                    def _():
                        pltpu.make_async_copy(src, dst, local_sem.at[9 + half]).start()
                else:
                    copy.start()
            return 0

        lax.fori_loop(0, 8, step, 0)

    for copy in keep_states:
        copy.wait()
    lax.fori_loop(0, 8, heard, 0)
    local(prompts, prompt_words, 11).wait()
    far_states(0)
    give(0)
    hop(1, y, 1, 5)
    landing(shared_at(0, x + 2, core, 0, 256), w_recv.at[2])
    landing(shared_at(0, x + 2, core, 256, 256), w_recv.at[3])
    to_sibling(shared_at(0, x + 2, core), 7)
    hop(1, y + 2, 3, 7)
    landing(direct_at(x + 3, core), x_recv.at[0])
    first = direct_at(x + 3, core, 0, 256)
    send(first, first, x_send.at[2], x_recv.at[2], x_up)
    to_sibling(direct_at(x + 3, core), 8)
    landing(direct_at(x + 1, core), x_recv.at[1])
    second = direct_at(x + 1, core, 256, 256)
    send(second, second, x_send.at[3], x_recv.at[3], x_down)
    to_sibling(direct_at(x + 1, core), 9)
    lax.fori_loop(3, 6, prepare, 0)
    far_states(1)
    give(1)
    for at in range(3):
        along_z(at)

    def multiply(weights_of, mine_to, theirs_to, theirs_in, slot):
        theirs_to[...] = dot_nn(rows[:count, :], weights_of[...])
        send(theirs_to, theirs_in, t_send.at[slot], t_recv.at[slot], partner)
        mine_to[...] = dot_nn(rows[count:, :], weights_of[...])

    def multiply_shared(step, slots):
        keep[step].wait()
        landing(shared_at(step, x, core + 1), d_recv.at[step])
        for dx, slot in zip(FAR, slots):
            landing(shared_at(step, x + dx, core + 1), d_recv.at[slot])
        multiply(shared.at[(z + step) % 4], total.at[step], partial.at[step], landed.at[step], step)

    landing(rows.at[pl.ds(0, count)], h_recv.at[0])
    keep_rows.wait()
    multiply_shared(0, (5, 6, 7))
    landing(direct_at(x + 2, core, 0, 256), x_recv.at[2])
    landing(direct_at(x + 2, core, 256, 256), x_recv.at[3])
    to_sibling(direct_at(x + 2, core), 10)
    lax.fori_loop(6, 8, prepare, 0)

    for at, dx in enumerate(FAR):
        landing(shared_at(3, x + dx, core), z_recv.at[at])
        first = shared_at(3, x + dx, core, 0, 256)
        send(first, first, z_send.at[6 + at], z_recv.at[6 + at], z_up)
        to_sibling(shared_at(3, x + dx, core), 11 + at)
        landing(shared_at(1, x + dx, core), z_recv.at[3 + at])
        second = shared_at(1, x + dx, core, 256, 256)
        send(second, second, z_send.at[9 + at], z_recv.at[9 + at], z_down)
        to_sibling(shared_at(1, x + dx, core), 14 + at)
        if at == 0:
            keep_direct.wait()
            landing(direct_at(x, core + 1), d_recv.at[4])
            for more, slot in zip(FAR, (8, 9, 10)):
                landing(direct_at(x + more, core + 1), d_recv.at[slot])
            multiply(direct, total_d, partial_d, landed_d, 4)
            lax.fori_loop(8, 11, prepare, 0)
        if at == 1:
            lax.fori_loop(11, 16, prepare, 0)
            leave = [local(inner, high_ref, 12), local(gate, low_ref, 13), local(gate_out, gate_out_ref, 14)]
    multiply_shared(3, (11, 12, 13))
    multiply_shared(1, (14, 15, 16))
    for at, dx in enumerate(FAR):
        landing(shared_at(2, x + dx, core, 0, 256), z_recv.at[6 + at])
        landing(shared_at(2, x + dx, core, 256, 256), z_recv.at[9 + at])
        to_sibling(shared_at(2, x + dx, core), 17 + at)
    multiply_shared(2, (17, 18, 19))

    landing(landed_d, t_recv.at[4])
    projected_ref[:, :DIRECT] = total_d[...] + landed_d[...]
    for step in (0, 3, 1, 2):
        landing(landed.at[step], t_recv.at[step])
        cols = pl.ds(pl.multiple_of(DIRECT + ((z + step) % 4) * SHARED, 128), SHARED)
        projected_ref[:, cols] = total[step] + landed[step]

    def settle(i, _):
        for half in range(2):
            @pl.when(i != me)
            def _():
                landing(arrived_ref.at[parity * 8 + i, pl.ds(*SPANS[0][half])], o_recv.at[half, 0, i])

            for kind in (1, 2):
                landing(arrived_ref.at[(1 - parity) * 8 + i, pl.ds(*SPANS[kind][half])], o_recv.at[half, kind, i])
            for kind in range(3):
                src = outgoing.at[min(kind, 1), i, pl.ds(*SPANS[kind][half])]
                copy = remote(src, src, o_send.at[half, kind, i], o_recv.at[half, kind, i], sibling)
                if kind == 0:
                    pl.when(i > 0)(copy.wait_send)
                else:
                    copy.wait_send()
        for kind in range(3):
            copy = remote(mine, mine, p_send.at[kind, i], p_recv.at[kind, i], sibling)
            if kind == 0:
                pl.when(i > 0)(copy.wait_send)
            else:
                copy.wait_send()
        return 0

    lax.fori_loop(0, 8, settle, 0)
    for half in range(2):
        span = pl.ds(*HALVES[half])
        pltpu.make_async_copy(outgoing.at[0, 0, span], arrived_ref.at[fsdp, span], local_sem.at[9 + half]).wait()
    for copy in leave:
        copy.wait()
    for copy in sent:
        copy.wait_send()


def exchange(
    hidden, weight, states, prompt, inner_raw, gate_raw, step_raw, decay_log, step_bias, conv_weight, conv_bias
):
    count, features = inner_raw.shape
    columns = weight.shape[1]
    heads = step_raw.shape[1]
    deep = PIECE + EXTRA
    dma = lambda *shape: pltpu.SemaphoreType.DMA(shape)
    anywhere = pl.BlockSpec(memory_space=pl.ANY)
    inside = pl.BlockSpec(memory_space=pltpu.VMEM)
    return pl.pallas_call(
        exchange_kernel,
        in_specs=[pl.BlockSpec(memory_space=pltpu.SMEM)] + [anywhere] * 5 + [inside] * 5,
        out_specs=[inside, anywhere, anywhere, anywhere, anywhere, inside],
        out_shape=[
            jax.ShapeDtypeStruct((count, columns), F32),
            jax.ShapeDtypeStruct((16, deep, 256), BF16),
            jax.ShapeDtypeStruct((count, features), BF16),
            jax.ShapeDtypeStruct((count, features), BF16),
            jax.ShapeDtypeStruct((count, features), F32),
            jax.ShapeDtypeStruct((HEAD_ROWS, features), F32),
        ],
        scratch_shapes=[
            pltpu.VMEM((4, 4096, SHARED), BF16),
            pltpu.VMEM((4096, DIRECT), BF16),
            pltpu.VMEM((2 * count, 4096), BF16),
            pltpu.VMEM((16, HALVES[0][1], 256), BF16),
            pltpu.VMEM((16, HALVES[1][1], 256), BF16),
            pltpu.VMEM((2, 8, deep, 256), BF16),
            pltpu.VMEM((3, 8, 8, 128), jnp.int32),
            pltpu.SMEM((3, 8, 8, 128), jnp.int32),
            pltpu.VMEM((4, count, SHARED), F32),
            pltpu.VMEM((4, count, SHARED), F32),
            pltpu.VMEM((4, count, SHARED), F32),
            pltpu.VMEM((count, DIRECT), F32),
            pltpu.VMEM((count, DIRECT), F32),
            pltpu.VMEM((count, DIRECT), F32),
            pltpu.VMEM((count, features), BF16),
            pltpu.VMEM((count, features), BF16),
            pltpu.VMEM((count, features), F32),
            pltpu.VMEM((count + 8, PIECE), F32),
            pltpu.VMEM((2 * heads, PIECE), jnp.int32),
            pltpu.VMEM((count, 2 * heads), BF16),
            pltpu.VMEM((count, 2 * heads), BF16),
            dma(4), dma(4), dma(4), dma(4), dma(12), dma(12), dma(20), dma(20), dma(2, 9), dma(2, 9),
            dma(2, 3, 8), dma(2, 3, 8), dma(3, 8), dma(3, 8), dma(1), dma(1), dma(5), dma(5), dma(16),
        ],
        compiler_params=pltpu.CompilerParams(
            collective_id=0, has_side_effects=True, vmem_limit_bytes=62 * 2**20
        ),
        cost_estimate=pl.CostEstimate(flops=9 * 10**9, bytes_accessed=2**25, transcendentals=0),
        name="exchange",
    )(prompt, hidden, weight, states, inner_raw, gate_raw, step_raw, decay_log, step_bias, conv_weight, conv_bias)


def on_device(
    hidden, inner_raw, gate_raw, step_raw, proj_weight, conv_weight, conv_bias, decay_log, step_bias,
    norm_gain, ssm_state, conv_state, slot_prompt, slot_len,
):
    conv_bias = conv_bias[None, :]
    part = lax.axis_index("fsdp")
    share = conv_state.shape[2] // 16
    prompts = conv_state.shape[0]
    piece = lax.dynamic_slice_in_dim(conv_state, part * share, share, axis=2).reshape(prompts, 3 * share)
    piece = jnp.pad(piece, ((0, 0), (0, EXTRA * 256 - 3 * share))).reshape(prompts, EXTRA, 256)
    own_states = jnp.concatenate([ssm_state.reshape(prompts, PIECE, 256), piece], axis=1)
    projected, state, high, low, gate, factor = exchange(
        hidden, proj_weight, own_states, slot_prompt, inner_raw, gate_raw, step_raw, decay_log[None, :],
        step_bias[None, :], conv_weight, conv_bias,
    )
    conv_rows = state[:, PIECE:, :].reshape(16, EXTRA * 256)[:, : 3 * share].reshape(16, 3, share)
    conv_rows = conv_rows.transpose(1, 0, 2).reshape(3, 16 * share)
    return after(
        slot_len, projected, conv_weight, conv_bias, conv_rows, state, inner_raw, factor, high, low, gate,
        norm_gain[None, :],
    )


def solution(mesh):
    rows = P(("dp", "fsdp"), None)
    in_specs = (
        rows, rows, rows, rows, P("fsdp", None), P(), P(), P(), P(), P(),
        P("dp", "fsdp", None, None), P("dp", None, None), P(("dp", "fsdp")), P(("dp", "fsdp")),
    )
    return jax.shard_map(on_device, mesh=mesh, in_specs=in_specs, out_specs=rows, check_vma=False)
```

```python
import jax
import jax.numpy as jnp
from jax import lax
from jax.experimental import pallas as pl
from jax.experimental.pallas import tpu as pltpu
from jax.sharding import PartitionSpec as P

F32 = jnp.float32
BF16 = jnp.bfloat16
PIECE = 512
HEAD_ROWS = 16


def split_two(value):
    high = value.astype(BF16)
    return high, (value - high.astype(F32)).astype(BF16)


def dot_nn(left, right):
    return jnp.dot(left, right, preferred_element_type=F32)


def dot_nt(left, right):
    return lax.dot_general(left, right, (((1,), (1,)), ((), ())), preferred_element_type=F32)


def silu(value):
    half = 0.5 * value
    return half + half * jnp.tanh(half)


def convolve(pad_ref, rows, first, taps, bias):
    count = rows.shape[0]
    pad_ref[5:8, :] = first
    pad_ref[8 : 8 + count, :] = rows
    total = taps[3:4, :] * rows + bias
    for k in range(3):
        total = total + taps[k : k + 1, :] * pad_ref[5 + k : 5 + k + count, :]
    return total


def after_kernel(
    length_ref, b_ref, c_ref, taps_ref, bias_ref, extra_ref, factor_ref, gain_ref, state_ref, inner_ref,
    high_ref, low_ref, gate_ref, out_ref, pad_ref, head_pad_ref, gated_ref, first_ref,
):
    count, n = b_ref.shape
    features = high_ref.shape[1]
    groups = gain_ref.shape[1] // features
    group = pl.program_id(0)

    @pl.when(group == 0)
    def _():
        share = first_ref.shape[1] // extra_ref.shape[0]
        for owner in range(extra_ref.shape[0]):
            held = extra_ref[owner].astype(F32)
            for at, low in enumerate(range(0, share, 256)):
                many = min(256, share - low)
                first_ref[0:3, owner * share + low : owner * share + low + many] = held[3 * at : 3 * at + 3, :many]

    def channel(pad, rows, low):
        cols = pl.ds(pl.multiple_of(low, 128), rows.shape[1])
        return silu(convolve(pad, rows[...].astype(F32), first_ref[0:3, cols], taps_ref[:, cols], bias_ref[:, cols]))

    wide = pl.ds(pl.multiple_of(group * features, features), features)
    head_rows = channel(head_pad_ref, inner_ref, group * features) * factor_ref[:, wide]
    head_high, head_low = split_two(head_rows)
    b_high, b_low = split_two(channel(pad_ref, b_ref, groups * features + group * n))
    c_high, c_low = split_two(channel(pad_ref, c_ref, groups * (features + n) + group * n))
    scores = dot_nt(c_high, b_high) + (dot_nt(c_high, b_low) + dot_nt(c_low, b_high))
    place = lax.broadcasted_iota(jnp.int32, (count, count), 0)
    other = lax.broadcasted_iota(jnp.int32, (count, count), 1)
    m_high, m_low = split_two(jnp.where(place >= other, scores, 0.0))
    squares = jnp.zeros((count, 128), F32)
    for low in range(0, features, PIECE):
        cols = slice(low, low + PIECE)
        state = state_ref[low // PIECE]
        high = jnp.concatenate([head_high[:, cols], high_ref[HEAD_ROWS:, cols]], axis=0)
        rest = jnp.concatenate([head_low[:, cols], low_ref[HEAD_ROWS:, cols]], axis=0)
        total = dot_nt(c_high, state) + dot_nt(c_low, state)
        total = total + dot_nn(m_high, high)
        total = total + (dot_nn(m_high, rest) + dot_nn(m_low, high))
        gated = total * gate_ref[:, cols]
        gated_ref[:, cols] = gated
        for at in range(0, PIECE, 128):
            part = gated[:, at : at + 128]
            squares = squares + part * part
    mean = jnp.sum(squares, axis=1, keepdims=True) * (1.0 / features)
    row = lax.broadcasted_iota(jnp.int32, (count, 1), 0)
    scale = jnp.where(row < length_ref[0], lax.rsqrt(mean + 1e-05), 0.0)
    gain = gain_ref[:, wide]
    for low in range(0, features, PIECE):
        cols = slice(low, low + PIECE)
        out_ref[:, cols] = (gated_ref[:, cols] * scale * gain[:, cols]).astype(BF16)


def after(
    length, projected, conv_weight, conv_bias, state, inner_raw, factor, high, low, gate, norm_gain
):
    count, features = high.shape
    n = state.shape[2]
    groups = projected.shape[1] // (2 * n)
    width = features // groups
    at = lambda base: pl.BlockSpec((count, n), lambda g: (0, base + g))
    wide = lambda rows: pl.BlockSpec((rows, width), lambda g: (0, g))
    whole = pl.BlockSpec(memory_space=pltpu.VMEM)
    return pl.pallas_call(
        after_kernel,
        grid=(groups,),
        in_specs=[
            pl.BlockSpec(memory_space=pltpu.SMEM),
            at(0), at(groups), whole, whole,
            pl.BlockSpec((16, EXTRA, n), lambda g: (0, PIECE // EXTRA, 0)), whole, whole,
            pl.BlockSpec((width // PIECE, PIECE, n), lambda g: (g, 0, 0)),
            wide(HEAD_ROWS), wide(count), wide(count), wide(count),
        ],
        out_specs=wide(count),
        out_shape=jax.ShapeDtypeStruct((count, features), BF16),
        scratch_shapes=[
            pltpu.VMEM((count + 8, n), F32),
            pltpu.VMEM((HEAD_ROWS + 8, width), F32),
            pltpu.VMEM((count, width), F32),
            pltpu.VMEM((8, conv_weight.shape[1]), F32),
        ],
        compiler_params=pltpu.CompilerParams(vmem_limit_bytes=62 * 2**20),
        name="scan_and_norm",
    )(
        length, projected, projected, conv_weight, conv_bias, state, factor, norm_gain, state,
        inner_raw, high, low, gate,
    )


EXTRA = 16
DIRECT = 512
SHARED = 384
MESH = pl.DeviceIdType.MESH
FAR = (3, 1, 2)
HALVES = ((0, 256), (256, 256 + EXTRA))
SPANS = (HALVES, ((0, 128), (256, 128)), ((128, 128), (384, 128 + EXTRA)))


def exchange_kernel(
    prompt_ref, hidden_ref, weight_ref, states_ref, inner_ref, gate_ref, step_ref, decay_ref,
    step_bias_ref, taps_ref, bias_ref, prompt_rows_ref,
    projected_ref, arrived_ref, high_ref, low_ref, gate_out_ref, factor_ref,
    shared, direct, rows, states_a, states_b, outgoing, prompts, prompt_words, partial, total, landed,
    partial_d, total_d, landed_d, inner, gate, gate_out, pad_ref, heads_ref, grow_ref, fall_ref,
    w_send, w_recv, x_send, x_recv, z_send, z_recv, d_send, d_recv, s_send, s_recv, o_send, o_recv,
    p_send, p_recv, h_send, h_recv, t_send, t_recv, local_sem,
):
    dp, fsdp = lax.axis_index("dp"), lax.axis_index("fsdp")
    z, x, core = dp % 4, (fsdp // 2) % 4, fsdp % 2
    y = (dp // 4) * 2 + fsdp // 8
    parity = y % 2
    depth = rows.shape[1]
    count = hidden_ref.shape[0]

    def device(xx, yy, zz, cc):
        xx, yy, zz, cc = xx % 4, yy % 4, zz % 4, cc % 2
        return ((yy // 2) * 4 + zz, ((yy % 2) * 4 + xx) * 2 + cc)

    sibling = device(x, y, z, core + 1)
    x_up, x_down = device(x + 1, y, z, core), device(x + 3, y, z, core)
    z_up, z_down = device(x, y, z + 1, core), device(x, y, z + 3, core)
    across = device(x, y + 2, z, core)
    partner = device(x, y + 1 + 2 * core, z, core + 1)

    def remote(src, dst, send, recv, to):
        return pltpu.make_async_remote_copy(
            src_ref=src, dst_ref=dst, send_sem=send, recv_sem=recv, device_id=to, device_id_type=MESH
        )

    sent = []

    def send(src, dst, send_sem, recv_sem, to):
        copy = remote(src, dst, send_sem, recv_sem, to)
        copy.start()
        sent.append(copy)

    def landing(dst, recv_sem):
        remote(dst, dst, recv_sem, recv_sem, sibling).wait_recv()

    def local(src, dst, at):
        copy = pltpu.make_async_copy(src, dst, local_sem.at[at])
        copy.start()
        return copy

    barrier = pltpu.get_barrier_semaphore()

    def greet(to):
        pl.semaphore_signal(barrier, inc=1, device_id=to, device_id_type=MESH)

    for dx in range(4):
        for dc in range(2):
            if dx or dc:
                greet(device(x + dx, y, z, core + dc))
            greet(device(x + dx, y + 1, z, core + dc))
            greet(device(x + dx, y + 3, z, core + dc))
    for to in (z_up, z_down, across):
        greet(to)
    keep_inner = local(inner_ref, inner, 0)
    keep_gate = local(gate_ref, gate, 1)
    me = x * 2 + core
    prompts[0, me] = jnp.full((8, 128), prompt_ref[0], jnp.int32)
    mine = prompts.at[0, me]
    pl.semaphore_wait(barrier, 26)

    states = (states_a, states_b)

    def unit(of, half):
        return states[half].at[pl.ds(2 * of, 2)]

    def one(of, which, half):
        return states[half].at[2 * of + which]

    def dp_at(yy, zz):
        return ((yy % 4) // 2) * 4 + zz % 4

    unit_here, unit_across = dp_at(y, z), dp_at(y + 2, z)

    def own_states(half, slot, to):
        src = states_ref.at[:, pl.ds(*HALVES[0])] if half == 0 else unit(unit_here, 1)
        send(src, unit(unit_here, half), s_send.at[half, slot], s_recv.at[half, slot], to)

    def own_along(half):
        own_states(half, 1, z_up)
        own_states(half, 2, z_down)

    def across_along(half):
        there = unit(unit_across, half)
        landing(there, s_recv.at[half, 0])
        send(there, there, s_send.at[half, 3], s_recv.at[half, 3], z_up)
        send(there, there, s_send.at[half, 4], s_recv.at[half, 4], z_down)

    def hop(half, yy, slot, onward):
        below, above = dp_at(yy, z + 3), dp_at(yy, z + 1)
        landing(unit(below, half), s_recv.at[half, slot])
        first = one(below, 0, half)
        send(first, first, s_send.at[half, onward], s_recv.at[half, onward], z_up)
        landing(unit(above, half), s_recv.at[half, slot + 1])
        second = one(above, 1, half)
        send(second, second, s_send.at[half, onward + 1], s_recv.at[half, onward + 1], z_down)

    def far_states(half):
        for yy, slot in ((y, 5), (y + 2, 7)):
            far = dp_at(yy, z + 2)
            landing(one(far, 0, half), s_recv.at[half, slot])
            landing(one(far, 1, half), s_recv.at[half, slot + 1])

    def block(xx, cc, low):
        return pl.multiple_of(((xx % 4) * 2 + cc % 2) * 512 + low, 256)

    def shared_at(step, xx, cc, low=0, many=512):
        return shared.at[(z + step) % 4, pl.ds(block(xx, cc, low), many)]

    def direct_at(xx, cc, low=0, many=512):
        return direct.at[pl.ds(block(xx, cc, low), many)]

    def own_shared(step):
        low = DIRECT + ((z + step) % 4) * SHARED
        return weight_ref.at[:, pl.ds(pl.multiple_of(low, 128), SHARED)]

    own_direct = weight_ref.at[:, pl.ds(0, DIRECT)]

    def to_sibling(ref, slot):
        send(ref, ref, d_send.at[slot], d_recv.at[slot], sibling)

    def along_z(at):
        whole = shared_at(0, x + FAR[at], core)
        send(whole, whole, z_send.at[at], z_recv.at[at], z_up)
        send(whole, whole, z_send.at[3 + at], z_recv.at[3 + at], z_down)

    def tell(i, _):
        dx, dc = i // 2, i % 2

        @pl.when(i > 0)
        def _():
            remote(mine, mine, p_send.at[0, i], p_recv.at[0, me], device(x + dx, y, z, core + dc)).start()

        remote(mine, prompts.at[2, me], p_send.at[1, i], p_recv.at[2, me], device(x + dx, y + 1, z, core + dc)).start()
        remote(mine, prompts.at[1, me], p_send.at[2, i], p_recv.at[1, me], device(x + dx, y + 3, z, core + dc)).start()
        return 0

    own_states(0, 0, across)
    own_along(0)
    send(own_shared(0), shared_at(0, x, core), w_send.at[0], w_recv.at[0], x_up)
    send(own_shared(0), shared_at(0, x, core), w_send.at[1], w_recv.at[1], x_down)
    lax.fori_loop(0, 8, tell, 0)
    keep_states = [
        local(states_ref.at[:, pl.ds(256 * half, 256)], unit(unit_here, half).at[:, pl.ds(0, 256)], (2, 15)[half])
        for half in range(2)
    ]
    share = prompt_rows_ref.shape[2] // 16
    for which in range(2):
        cols = pl.ds(pl.multiple_of(fsdp * share, 128), share)
        held = [prompt_rows_ref[tap, :, cols].astype(F32)[which : which + 1] for tap in range(3)]
        held = jnp.concatenate(held, axis=0)
        parts = [held[:, low : min(low + 256, share)] for low in range(0, share, 256)]
        parts[-1] = jnp.concatenate([parts[-1], jnp.zeros((3, 256 - parts[-1].shape[1]), F32)], axis=1)
        parts.append(jnp.zeros((EXTRA - 3 * len(parts), 256), F32))
        states_b[2 * unit_here + which, pl.ds(256, EXTRA)] = jnp.concatenate(parts, axis=0).astype(BF16)
    theirs = pl.ds(pl.multiple_of((1 - parity) * depth, depth), depth)
    ours = pl.ds(pl.multiple_of(parity * depth, depth), depth)
    keep_rows = local(hidden_ref.at[:, ours], rows.at[pl.ds(count, count)], 3)
    keep = {}
    for step in (0, 1, 3, 2):
        send(own_shared(step), shared_at(step, x, core), d_send.at[step], d_recv.at[step], sibling)
        keep[step] = local(own_shared(step), shared_at(step, x, core), 4 + step)
    send(own_direct, direct_at(x, core), d_send.at[4], d_recv.at[4], sibling)
    keep_direct = local(own_direct, direct_at(x, core), 8)

    heads = step_ref.shape[1]

    def decays():
        raw = step_ref[...] + step_bias_ref[...]
        steps = jnp.maximum(raw, 0.0) + jnp.log1p(jnp.exp(-jnp.abs(raw)))
        logs = -jnp.exp(decay_ref[...]) * steps
        place = lax.broadcasted_iota(jnp.int32, (count, count), 0)
        other = lax.broadcasted_iota(jnp.int32, (count, count), 1)
        lower = jnp.where(place >= other, 1.0, 0.0).astype(BF16)
        top = logs.astype(BF16)
        mid, last = split_two(logs - top.astype(F32))
        summed = dot_nn(lower, top) + (dot_nn(lower, mid) + dot_nn(lower, last))
        grow_ref[:, :heads], grow_ref[:, heads:] = split_two(steps * jnp.exp(-summed))
        fall_ref[:, :heads], fall_ref[:, heads:] = split_two(jnp.exp(summed))
        head = lax.broadcasted_iota(jnp.int32, (2 * heads, PIECE), 0)
        column = lax.broadcasted_iota(jnp.int32, (2 * heads, PIECE), 1)
        heads_ref[...] = jnp.where(head >= heads, head - heads, head) - column // 64

    def prepare(tile, _):
        cols = pl.ds(pl.multiple_of(tile * PIECE, PIECE), PIECE)
        spread = jnp.where(heads_ref[...] == tile * (PIECE // 64), 1.0, 0.0).astype(BF16)
        factor = dot_nn(grow_ref[...], spread)
        factor_ref[:, cols] = factor[:HEAD_ROWS, :]
        none = jnp.zeros((3, PIECE), F32)
        active = silu(convolve(pad_ref, inner[:, cols].astype(F32), none, taps_ref[:, cols], bias_ref[:, cols]))
        gate_out[:, cols] = silu(gate[:, cols].astype(F32)) * dot_nn(fall_ref[...], spread)
        inner[:, cols], gate[:, cols] = split_two(active * factor)
        return 0

    keep_inner.wait()
    keep_gate.wait()
    decays()
    lax.fori_loop(0, 3, prepare, 0)

    across_along(0)
    for copy in keep_states:
        copy.wait()
    own_states(1, 0, across)
    hop(0, y, 1, 5)
    landing(shared_at(0, x + 3, core), w_recv.at[0])
    first = shared_at(0, x + 3, core, 0, 256)
    send(first, first, w_send.at[2], w_recv.at[2], x_up)
    to_sibling(shared_at(0, x + 3, core), 5)
    landing(shared_at(0, x + 1, core), w_recv.at[1])
    second = shared_at(0, x + 1, core, 256, 256)
    send(second, second, w_send.at[3], w_recv.at[3], x_down)
    to_sibling(shared_at(0, x + 1, core), 6)
    send(own_direct, direct_at(x, core), x_send.at[0], x_recv.at[0], x_up)
    send(own_direct, direct_at(x, core), x_send.at[1], x_recv.at[1], x_down)
    hop(0, y + 2, 3, 7)
    own_along(1)
    across_along(1)
    send(hidden_ref.at[:, theirs], rows.at[pl.ds(0, count)], h_send.at[0], h_recv.at[0], partner)

    def heard(i, _):
        @pl.when(i != me)
        def _():
            landing(prompts.at[0, i], p_recv.at[0, i])

        landing(prompts.at[1, i], p_recv.at[1, i])
        landing(prompts.at[2, i], p_recv.at[2, i])
        return 0

    def give(half):
        def step(i, _):
            to_x, to_core = (x + i // 2) % 4, (core + i % 2) % 2
            at = to_x * 2 + to_core
            for kind in range(3):
                low, size = SPANS[kind][half]
                span = pl.ds(low, size)
                outgoing[min(kind, 1), i, span] = states[half][
                    prompt_words[kind, at, 0, 0], pl.ds(low - HALVES[half][0], size)
                ]
                src = outgoing.at[min(kind, 1), i, span]
                dst = arrived_ref.at[fsdp, span]
                copy = remote(
                    src, dst, o_send.at[half, kind, i], o_recv.at[half, kind, me],
                    device(to_x, y + (0, 1, 3)[kind], z, to_core),
                )
                if kind == 0:
                    pl.when(i > 0)(copy.start)

                    @pl.when(i == 0)
                    def _():
                        pltpu.make_async_copy(src, dst, local_sem.at[9 + half]).start()
                else:
                    copy.start()
            return 0

        lax.fori_loop(0, 8, step, 0)

    lax.fori_loop(0, 8, heard, 0)
    local(prompts, prompt_words, 11).wait()
    far_states(0)
    give(0)
    hop(1, y, 1, 5)
    along_z(0)
    along_z(1)
    landing(shared_at(0, x + 2, core, 0, 256), w_recv.at[2])
    landing(shared_at(0, x + 2, core, 256, 256), w_recv.at[3])
    to_sibling(shared_at(0, x + 2, core), 7)
    hop(1, y + 2, 3, 7)
    landing(direct_at(x + 3, core), x_recv.at[0])
    first = direct_at(x + 3, core, 0, 256)
    send(first, first, x_send.at[2], x_recv.at[2], x_up)
    to_sibling(direct_at(x + 3, core), 8)
    landing(direct_at(x + 1, core), x_recv.at[1])
    second = direct_at(x + 1, core, 256, 256)
    send(second, second, x_send.at[3], x_recv.at[3], x_down)
    to_sibling(direct_at(x + 1, core), 9)
    lax.fori_loop(3, 6, prepare, 0)
    along_z(2)
    far_states(1)
    give(1)

    def multiply(weights_of, mine_to, theirs_to, theirs_in, slot):
        theirs_to[...] = dot_nn(rows[:count, :], weights_of[...])
        send(theirs_to, theirs_in, t_send.at[slot], t_recv.at[slot], partner)
        mine_to[...] = dot_nn(rows[count:, :], weights_of[...])

    def multiply_shared(step, slots):
        keep[step].wait()
        landing(shared_at(step, x, core + 1), d_recv.at[step])
        for dx, slot in zip(FAR, slots):
            landing(shared_at(step, x + dx, core + 1), d_recv.at[slot])
        multiply(shared.at[(z + step) % 4], total.at[step], partial.at[step], landed.at[step], step)

    landing(rows.at[pl.ds(0, count)], h_recv.at[0])
    keep_rows.wait()
    multiply_shared(0, (5, 6, 7))
    landing(direct_at(x + 2, core, 0, 256), x_recv.at[2])
    landing(direct_at(x + 2, core, 256, 256), x_recv.at[3])
    to_sibling(direct_at(x + 2, core), 10)
    lax.fori_loop(6, 8, prepare, 0)

    for at, dx in enumerate(FAR):
        landing(shared_at(3, x + dx, core), z_recv.at[at])
        first = shared_at(3, x + dx, core, 0, 256)
        send(first, first, z_send.at[6 + at], z_recv.at[6 + at], z_up)
        to_sibling(shared_at(3, x + dx, core), 11 + at)
        landing(shared_at(1, x + dx, core), z_recv.at[3 + at])
        second = shared_at(1, x + dx, core, 256, 256)
        send(second, second, z_send.at[9 + at], z_recv.at[9 + at], z_down)
        to_sibling(shared_at(1, x + dx, core), 14 + at)
        if at == 0:
            keep_direct.wait()
            landing(direct_at(x, core + 1), d_recv.at[4])
            for more, slot in zip(FAR, (8, 9, 10)):
                landing(direct_at(x + more, core + 1), d_recv.at[slot])
            multiply(direct, total_d, partial_d, landed_d, 4)
            lax.fori_loop(8, 11, prepare, 0)
        if at == 1:
            lax.fori_loop(11, 16, prepare, 0)
            leave = [local(inner, high_ref, 12), local(gate, low_ref, 13), local(gate_out, gate_out_ref, 14)]
    multiply_shared(3, (11, 12, 13))
    multiply_shared(1, (14, 15, 16))
    def last_part(xx, start, finish):
        deep = pl.ds(pl.multiple_of((xx % 4) * 1024, 1024), 1024)
        piece = shared[(z + 2) % 4, deep]
        theirs_now = dot_nn(rows[:count, deep], piece)
        partial[2] = theirs_now if start else partial[2] + theirs_now
        if finish:
            send(partial.at[2], landed.at[2], t_send.at[2], t_recv.at[2], partner)
        own_now = dot_nn(rows[count:, deep], piece)
        total[2] = own_now if start else total[2] + own_now

    def last_lands(at):
        here = x + FAR[at]
        landing(shared_at(2, here, core, 0, 256), z_recv.at[6 + at])
        landing(shared_at(2, here, core, 256, 256), z_recv.at[9 + at])
        to_sibling(shared_at(2, here, core), 17 + at)

    keep[2].wait()
    landing(shared_at(2, x, core + 1), d_recv.at[2])
    last_part(x, True, False)
    last_lands(0)
    last_lands(1)
    landing(shared_at(2, x + FAR[0], core + 1), d_recv.at[17])
    last_part(x + FAR[0], False, False)
    last_lands(2)
    landing(shared_at(2, x + FAR[1], core + 1), d_recv.at[18])
    last_part(x + FAR[1], False, False)
    landing(shared_at(2, x + FAR[2], core + 1), d_recv.at[19])
    last_part(x + FAR[2], False, True)

    landing(landed_d, t_recv.at[4])
    projected_ref[:, :DIRECT] = total_d[...] + landed_d[...]
    for step in (0, 3, 1, 2):
        landing(landed.at[step], t_recv.at[step])
        cols = pl.ds(pl.multiple_of(DIRECT + ((z + step) % 4) * SHARED, 128), SHARED)
        projected_ref[:, cols] = total[step] + landed[step]

    def settle(i, _):
        for half in range(2):
            @pl.when(i != me)
            def _():
                landing(arrived_ref.at[parity * 8 + i, pl.ds(*SPANS[0][half])], o_recv.at[half, 0, i])

            for kind in (1, 2):
                landing(arrived_ref.at[(1 - parity) * 8 + i, pl.ds(*SPANS[kind][half])], o_recv.at[half, kind, i])
            for kind in range(3):
                src = outgoing.at[min(kind, 1), i, pl.ds(*SPANS[kind][half])]
                copy = remote(src, src, o_send.at[half, kind, i], o_recv.at[half, kind, i], sibling)
                if kind == 0:
                    pl.when(i > 0)(copy.wait_send)
                else:
                    copy.wait_send()
        for kind in range(3):
            copy = remote(mine, mine, p_send.at[kind, i], p_recv.at[kind, i], sibling)
            if kind == 0:
                pl.when(i > 0)(copy.wait_send)
            else:
                copy.wait_send()
        return 0

    lax.fori_loop(0, 8, settle, 0)
    for half in range(2):
        span = pl.ds(*HALVES[half])
        pltpu.make_async_copy(outgoing.at[0, 0, span], arrived_ref.at[fsdp, span], local_sem.at[9 + half]).wait()
    for copy in leave:
        copy.wait()
    for copy in sent:
        copy.wait_send()


def exchange(
    hidden, weight, states, conv_state, prompt, inner_raw, gate_raw, step_raw, decay_log, step_bias, conv_weight, conv_bias
):
    count, features = inner_raw.shape
    columns = weight.shape[1]
    heads = step_raw.shape[1]
    deep = PIECE + EXTRA
    dma = lambda *shape: pltpu.SemaphoreType.DMA(shape)
    anywhere = pl.BlockSpec(memory_space=pl.ANY)
    inside = pl.BlockSpec(memory_space=pltpu.VMEM)
    return pl.pallas_call(
        exchange_kernel,
        in_specs=[pl.BlockSpec(memory_space=pltpu.SMEM)] + [anywhere] * 5 + [inside] * 6,
        out_specs=[inside, anywhere, anywhere, anywhere, anywhere, inside],
        out_shape=[
            jax.ShapeDtypeStruct((count, columns), F32),
            jax.ShapeDtypeStruct((16, deep, 256), BF16),
            jax.ShapeDtypeStruct((count, features), BF16),
            jax.ShapeDtypeStruct((count, features), BF16),
            jax.ShapeDtypeStruct((count, features), F32),
            jax.ShapeDtypeStruct((HEAD_ROWS, features), F32),
        ],
        scratch_shapes=[
            pltpu.VMEM((4, 4096, SHARED), BF16),
            pltpu.VMEM((4096, DIRECT), BF16),
            pltpu.VMEM((2 * count, 4096), BF16),
            pltpu.VMEM((16, HALVES[0][1], 256), BF16),
            pltpu.VMEM((16, HALVES[1][1], 256), BF16),
            pltpu.VMEM((2, 8, deep, 256), BF16),
            pltpu.VMEM((3, 8, 8, 128), jnp.int32),
            pltpu.SMEM((3, 8, 8, 128), jnp.int32),
            pltpu.VMEM((4, count, SHARED), F32),
            pltpu.VMEM((4, count, SHARED), F32),
            pltpu.VMEM((4, count, SHARED), F32),
            pltpu.VMEM((count, DIRECT), F32),
            pltpu.VMEM((count, DIRECT), F32),
            pltpu.VMEM((count, DIRECT), F32),
            pltpu.VMEM((count, features), BF16),
            pltpu.VMEM((count, features), BF16),
            pltpu.VMEM((count, features), F32),
            pltpu.VMEM((count + 8, PIECE), F32),
            pltpu.VMEM((2 * heads, PIECE), jnp.int32),
            pltpu.VMEM((count, 2 * heads), BF16),
            pltpu.VMEM((count, 2 * heads), BF16),
            dma(4), dma(4), dma(4), dma(4), dma(12), dma(12), dma(20), dma(20), dma(2, 9), dma(2, 9),
            dma(2, 3, 8), dma(2, 3, 8), dma(3, 8), dma(3, 8), dma(1), dma(1), dma(5), dma(5), dma(16),
        ],
        compiler_params=pltpu.CompilerParams(
            collective_id=0, has_side_effects=True, vmem_limit_bytes=62 * 2**20
        ),
        cost_estimate=pl.CostEstimate(flops=9 * 10**9, bytes_accessed=2**25, transcendentals=0),
        name="exchange",
    )(
        prompt, hidden, weight, states, inner_raw, gate_raw, step_raw, decay_log, step_bias, conv_weight,
        conv_bias, conv_state.transpose(1, 0, 2),
    )


def on_device(
    hidden, inner_raw, gate_raw, step_raw, proj_weight, conv_weight, conv_bias, decay_log, step_bias,
    norm_gain, ssm_state, conv_state, slot_prompt, slot_len,
):
    conv_bias = conv_bias[None, :]
    own_states = ssm_state.reshape(ssm_state.shape[0], PIECE, ssm_state.shape[3])
    projected, state, high, low, gate, factor = exchange(
        hidden, proj_weight, own_states, conv_state, slot_prompt, inner_raw, gate_raw, step_raw, decay_log[None, :],
        step_bias[None, :], conv_weight, conv_bias,
    )
    return after(
        slot_len, projected, conv_weight, conv_bias, state, inner_raw, factor, high, low, gate,
        norm_gain[None, :],
    )


def solution(mesh):
    rows = P(("dp", "fsdp"), None)
    in_specs = (
        rows, rows, rows, rows, P("fsdp", None), P(), P(), P(), P(), P(),
        P("dp", "fsdp", None, None), P("dp", None, None), P(("dp", "fsdp")), P(("dp", "fsdp")),
    )
    return jax.shard_map(on_device, mesh=mesh, in_specs=in_specs, out_specs=rows, check_vma=False)
```

```python
import jax
import jax.numpy as jnp
from jax import lax
from jax.experimental import pallas as pl
from jax.experimental.pallas import tpu as pltpu
from jax.sharding import PartitionSpec as P

F32 = jnp.float32
BF16 = jnp.bfloat16
PIECE = 512
HEAD_ROWS = 16


def split_two(value):
    high = value.astype(BF16)
    return high, (value - high.astype(F32)).astype(BF16)


def dot_nn(left, right):
    return jnp.dot(left, right, preferred_element_type=F32)


def dot_nt(left, right):
    return lax.dot_general(left, right, (((1,), (1,)), ((), ())), preferred_element_type=F32)


def silu(value):
    half = 0.5 * value
    return half + half * jnp.tanh(half)


def convolve(pad_ref, rows, first, taps, bias):
    count = rows.shape[0]
    pad_ref[5:8, :] = first
    pad_ref[8 : 8 + count, :] = rows
    total = taps[3:4, :] * rows + bias
    for k in range(3):
        total = total + taps[k : k + 1, :] * pad_ref[5 + k : 5 + k + count, :]
    return total


def after_kernel(
    length_ref, b_ref, c_ref, taps_ref, bias_ref, extra_ref, factor_ref, gain_ref, state_ref, inner_ref,
    high_ref, low_ref, gate_ref, out_ref, pad_ref, head_pad_ref, gated_ref, first_ref,
):
    count, n = b_ref.shape
    features = high_ref.shape[1]
    groups = gain_ref.shape[1] // features
    group = pl.program_id(0)

    @pl.when(group == 0)
    def _():
        share = first_ref.shape[1] // extra_ref.shape[0]
        for owner in range(extra_ref.shape[0]):
            held = extra_ref[owner].astype(F32)
            for at, low in enumerate(range(0, share, 256)):
                many = min(256, share - low)
                first_ref[0:3, owner * share + low : owner * share + low + many] = held[3 * at : 3 * at + 3, :many]

    def channel(pad, rows, low):
        cols = pl.ds(pl.multiple_of(low, 128), rows.shape[1])
        return silu(convolve(pad, rows[...].astype(F32), first_ref[0:3, cols], taps_ref[:, cols], bias_ref[:, cols]))

    wide = pl.ds(pl.multiple_of(group * features, features), features)
    head_rows = channel(head_pad_ref, inner_ref, group * features) * factor_ref[:, wide]
    head_high, head_low = split_two(head_rows)
    b_high, b_low = split_two(channel(pad_ref, b_ref, groups * features + group * n))
    c_high, c_low = split_two(channel(pad_ref, c_ref, groups * (features + n) + group * n))
    scores = dot_nt(c_high, b_high) + (dot_nt(c_high, b_low) + dot_nt(c_low, b_high))
    place = lax.broadcasted_iota(jnp.int32, (count, count), 0)
    other = lax.broadcasted_iota(jnp.int32, (count, count), 1)
    m_high, m_low = split_two(jnp.where(place >= other, scores, 0.0))
    squares = jnp.zeros((count, 128), F32)
    for low in range(0, features, PIECE):
        cols = slice(low, low + PIECE)
        state = state_ref[low // PIECE]
        high = jnp.concatenate([head_high[:, cols], high_ref[HEAD_ROWS:, cols]], axis=0)
        rest = jnp.concatenate([head_low[:, cols], low_ref[HEAD_ROWS:, cols]], axis=0)
        total = dot_nt(c_high, state) + dot_nt(c_low, state)
        total = total + dot_nn(m_high, high)
        total = total + (dot_nn(m_high, rest) + dot_nn(m_low, high))
        gated = total * gate_ref[:, cols]
        gated_ref[:, cols] = gated
        for at in range(0, PIECE, 128):
            part = gated[:, at : at + 128]
            squares = squares + part * part
    mean = jnp.sum(squares, axis=1, keepdims=True) * (1.0 / features)
    row = lax.broadcasted_iota(jnp.int32, (count, 1), 0)
    scale = jnp.where(row < length_ref[0], lax.rsqrt(mean + 1e-05), 0.0)
    gain = gain_ref[:, wide]
    for low in range(0, features, PIECE):
        cols = slice(low, low + PIECE)
        out_ref[:, cols] = (gated_ref[:, cols] * scale * gain[:, cols]).astype(BF16)


def after(
    length, projected, conv_weight, conv_bias, state, inner_raw, factor, high, low, gate, norm_gain
):
    count, features = high.shape
    n = state.shape[2]
    groups = projected.shape[1] // (2 * n)
    width = features // groups
    at = lambda base: pl.BlockSpec((count, n), lambda g: (0, base + g))
    wide = lambda rows: pl.BlockSpec((rows, width), lambda g: (0, g))
    whole = pl.BlockSpec(memory_space=pltpu.VMEM)
    return pl.pallas_call(
        after_kernel,
        grid=(groups,),
        in_specs=[
            pl.BlockSpec(memory_space=pltpu.SMEM),
            at(0), at(groups), whole, whole,
            pl.BlockSpec((16, EXTRA, n), lambda g: (0, PIECE // EXTRA, 0)), whole, whole,
            pl.BlockSpec((width // PIECE, PIECE, n), lambda g: (g, 0, 0)),
            wide(HEAD_ROWS), wide(count), wide(count), wide(count),
        ],
        out_specs=wide(count),
        out_shape=jax.ShapeDtypeStruct((count, features), BF16),
        scratch_shapes=[
            pltpu.VMEM((count + 8, n), F32),
            pltpu.VMEM((HEAD_ROWS + 8, width), F32),
            pltpu.VMEM((count, width), F32),
            pltpu.VMEM((8, conv_weight.shape[1]), F32),
        ],
        compiler_params=pltpu.CompilerParams(vmem_limit_bytes=62 * 2**20),
        name="scan_and_norm",
    )(
        length, projected, projected, conv_weight, conv_bias, state, factor, norm_gain, state,
        inner_raw, high, low, gate,
    )


EXTRA = 16
DIRECT = 512
SHARED = 384
MESH = pl.DeviceIdType.MESH
FAR = (3, 1, 2)
HALVES = ((0, 256), (256, 256 + EXTRA))
SPANS = (HALVES, ((0, 128), (256, 128)), ((128, 128), (384, 128 + EXTRA)))


def exchange_kernel(
    prompt_ref, hidden_ref, weight_ref, states_ref, inner_ref, gate_ref, step_ref, decay_ref,
    step_bias_ref, taps_ref, bias_ref, prompt_rows_ref,
    projected_ref, arrived_ref, high_ref, low_ref, gate_out_ref, factor_ref,
    shared, direct, rows, states_a, states_b, outgoing, prompts, prompt_words, partial, total, landed,
    partial_d, total_d, landed_d, inner, gate, gate_out, pad_ref, heads_ref, grow_ref, fall_ref,
    w_send, w_recv, x_send, x_recv, z_send, z_recv, d_send, d_recv, s_send, s_recv, o_send, o_recv,
    p_send, p_recv, h_send, h_recv, t_send, t_recv, local_sem,
):
    dp, fsdp = lax.axis_index("dp"), lax.axis_index("fsdp")
    z, x, core = dp % 4, (fsdp // 2) % 4, fsdp % 2
    y = (dp // 4) * 2 + fsdp // 8
    parity = y % 2
    depth = rows.shape[1]
    count = hidden_ref.shape[0]

    def device(xx, yy, zz, cc):
        xx, yy, zz, cc = xx % 4, yy % 4, zz % 4, cc % 2
        return ((yy // 2) * 4 + zz, ((yy % 2) * 4 + xx) * 2 + cc)

    sibling = device(x, y, z, core + 1)
    x_up, x_down = device(x + 1, y, z, core), device(x + 3, y, z, core)
    z_up, z_down = device(x, y, z + 1, core), device(x, y, z + 3, core)
    across = device(x, y + 2, z, core)
    partner = device(x, y + 1 + 2 * core, z, core + 1)

    def remote(src, dst, send, recv, to):
        return pltpu.make_async_remote_copy(
            src_ref=src, dst_ref=dst, send_sem=send, recv_sem=recv, device_id=to, device_id_type=MESH
        )

    sent = []

    def send(src, dst, send_sem, recv_sem, to):
        copy = remote(src, dst, send_sem, recv_sem, to)
        copy.start()
        sent.append(copy)

    def landing(dst, recv_sem):
        remote(dst, dst, recv_sem, recv_sem, sibling).wait_recv()

    def local(src, dst, at):
        copy = pltpu.make_async_copy(src, dst, local_sem.at[at])
        copy.start()
        return copy

    barrier = pltpu.get_barrier_semaphore()

    def greet(to):
        pl.semaphore_signal(barrier, inc=1, device_id=to, device_id_type=MESH)

    for dx in range(4):
        for dc in range(2):
            if dx or dc:
                greet(device(x + dx, y, z, core + dc))
            greet(device(x + dx, y + 1, z, core + dc))
            greet(device(x + dx, y + 3, z, core + dc))
    for to in (z_up, z_down, across):
        greet(to)
    keep_inner = local(inner_ref, inner, 0)
    keep_gate = local(gate_ref, gate, 1)
    me = x * 2 + core
    prompts[0, me] = jnp.full((8, 128), prompt_ref[0], jnp.int32)
    mine = prompts.at[0, me]
    pl.semaphore_wait(barrier, 26)

    states = (states_a, states_b)

    def unit(of, half):
        return states[half].at[pl.ds(2 * of, 2)]

    def one(of, which, half):
        return states[half].at[2 * of + which]

    def dp_at(yy, zz):
        return ((yy % 4) // 2) * 4 + zz % 4

    unit_here, unit_across = dp_at(y, z), dp_at(y + 2, z)

    def own_states(half, slot, to):
        src = states_ref.at[:, pl.ds(*HALVES[0])] if half == 0 else unit(unit_here, 1)
        send(src, unit(unit_here, half), s_send.at[half, slot], s_recv.at[half, slot], to)

    def own_along(half):
        own_states(half, 1, z_up)
        own_states(half, 2, z_down)

    def across_along(half):
        there = unit(unit_across, half)
        landing(there, s_recv.at[half, 0])
        send(there, there, s_send.at[half, 3], s_recv.at[half, 3], z_up)
        send(there, there, s_send.at[half, 4], s_recv.at[half, 4], z_down)

    def hop(half, yy, slot, onward):
        below, above = dp_at(yy, z + 3), dp_at(yy, z + 1)
        landing(unit(below, half), s_recv.at[half, slot])
        first = one(below, 0, half)
        send(first, first, s_send.at[half, onward], s_recv.at[half, onward], z_up)
        landing(unit(above, half), s_recv.at[half, slot + 1])
        second = one(above, 1, half)
        send(second, second, s_send.at[half, onward + 1], s_recv.at[half, onward + 1], z_down)

    def far_states(half):
        for yy, slot in ((y, 5), (y + 2, 7)):
            far = dp_at(yy, z + 2)
            landing(one(far, 0, half), s_recv.at[half, slot])
            landing(one(far, 1, half), s_recv.at[half, slot + 1])

    def block(xx, cc, low):
        return pl.multiple_of(((xx % 4) * 2 + cc % 2) * 512 + low, 256)

    def shared_at(step, xx, cc, low=0, many=512):
        return shared.at[(z + step) % 4, pl.ds(block(xx, cc, low), many)]

    def direct_at(xx, cc, low=0, many=512):
        return direct.at[pl.ds(block(xx, cc, low), many)]

    def own_shared(step):
        low = DIRECT + ((z + step) % 4) * SHARED
        return weight_ref.at[:, pl.ds(pl.multiple_of(low, 128), SHARED)]

    own_direct = weight_ref.at[:, pl.ds(0, DIRECT)]

    def to_sibling(ref, slot):
        send(ref, ref, d_send.at[slot], d_recv.at[slot], sibling)

    def along_z(at):
        whole = shared_at(0, x + FAR[at], core)
        send(whole, whole, z_send.at[at], z_recv.at[at], z_up)
        send(whole, whole, z_send.at[3 + at], z_recv.at[3 + at], z_down)

    def tell(i, _):
        dx, dc = i // 2, i % 2

        @pl.when(i > 0)
        def _():
            remote(mine, mine, p_send.at[0, i], p_recv.at[0, me], device(x + dx, y, z, core + dc)).start()

        remote(mine, prompts.at[2, me], p_send.at[1, i], p_recv.at[2, me], device(x + dx, y + 1, z, core + dc)).start()
        remote(mine, prompts.at[1, me], p_send.at[2, i], p_recv.at[1, me], device(x + dx, y + 3, z, core + dc)).start()
        return 0

    own_states(0, 0, across)
    own_along(0)
    send(own_shared(0), shared_at(0, x, core), w_send.at[0], w_recv.at[0], x_up)
    send(own_shared(0), shared_at(0, x, core), w_send.at[1], w_recv.at[1], x_down)
    lax.fori_loop(0, 8, tell, 0)
    keep_states = [
        local(states_ref.at[:, pl.ds(256 * half, 256)], unit(unit_here, half).at[:, pl.ds(0, 256)], (2, 15)[half])
        for half in range(2)
    ]
    share = prompt_rows_ref.shape[2] // 16
    for which in range(2):
        cols = pl.ds(pl.multiple_of(fsdp * share, 128), share)
        held = [prompt_rows_ref[tap, :, cols].astype(F32)[which : which + 1] for tap in range(3)]
        held = jnp.concatenate(held, axis=0)
        parts = [held[:, low : min(low + 256, share)] for low in range(0, share, 256)]
        parts[-1] = jnp.concatenate([parts[-1], jnp.zeros((3, 256 - parts[-1].shape[1]), F32)], axis=1)
        parts.append(jnp.zeros((EXTRA - 3 * len(parts), 256), F32))
        states_b[2 * unit_here + which, pl.ds(256, EXTRA)] = jnp.concatenate(parts, axis=0).astype(BF16)
    theirs = pl.ds(pl.multiple_of((1 - parity) * depth, depth), depth)
    ours = pl.ds(pl.multiple_of(parity * depth, depth), depth)
    keep_rows = local(hidden_ref.at[:, ours], rows.at[pl.ds(count, count)], 3)
    keep = {}
    for step in (0, 1, 3, 2):
        send(own_shared(step), shared_at(step, x, core), d_send.at[step], d_recv.at[step], sibling)
        keep[step] = local(own_shared(step), shared_at(step, x, core), 4 + step)
    send(own_direct, direct_at(x, core), d_send.at[4], d_recv.at[4], sibling)
    keep_direct = local(own_direct, direct_at(x, core), 8)

    heads = step_ref.shape[1]

    def decays():
        raw = step_ref[...] + step_bias_ref[...]
        steps = jnp.maximum(raw, 0.0) + jnp.log1p(jnp.exp(-jnp.abs(raw)))
        logs = -jnp.exp(decay_ref[...]) * steps
        place = lax.broadcasted_iota(jnp.int32, (count, count), 0)
        other = lax.broadcasted_iota(jnp.int32, (count, count), 1)
        lower = jnp.where(place >= other, 1.0, 0.0).astype(BF16)
        top = logs.astype(BF16)
        mid, last = split_two(logs - top.astype(F32))
        summed = dot_nn(lower, top) + (dot_nn(lower, mid) + dot_nn(lower, last))
        grow_ref[:, :heads], grow_ref[:, heads:] = split_two(steps * jnp.exp(-summed))
        fall_ref[:, :heads], fall_ref[:, heads:] = split_two(jnp.exp(summed))
        head = lax.broadcasted_iota(jnp.int32, (2 * heads, PIECE), 0)
        column = lax.broadcasted_iota(jnp.int32, (2 * heads, PIECE), 1)
        heads_ref[...] = jnp.where(head >= heads, head - heads, head) - column // 64

    def prepare(tile, _):
        cols = pl.ds(pl.multiple_of(tile * PIECE, PIECE), PIECE)
        spread = jnp.where(heads_ref[...] == tile * (PIECE // 64), 1.0, 0.0).astype(BF16)
        factor = dot_nn(grow_ref[...], spread)
        factor_ref[:, cols] = factor[:HEAD_ROWS, :]
        none = jnp.zeros((3, PIECE), F32)
        active = silu(convolve(pad_ref, inner[:, cols].astype(F32), none, taps_ref[:, cols], bias_ref[:, cols]))
        gate_out[:, cols] = silu(gate[:, cols].astype(F32)) * dot_nn(fall_ref[...], spread)
        inner[:, cols], gate[:, cols] = split_two(active * factor)
        return 0

    keep_inner.wait()
    keep_gate.wait()
    decays()
    lax.fori_loop(0, 3, prepare, 0)

    across_along(0)
    for copy in keep_states:
        copy.wait()
    own_states(1, 0, across)
    hop(0, y, 1, 5)
    landing(shared_at(0, x + 3, core), w_recv.at[0])
    first = shared_at(0, x + 3, core, 0, 256)
    send(first, first, w_send.at[2], w_recv.at[2], x_up)
    to_sibling(shared_at(0, x + 3, core), 5)
    landing(shared_at(0, x + 1, core), w_recv.at[1])
    second = shared_at(0, x + 1, core, 256, 256)
    send(second, second, w_send.at[3], w_recv.at[3], x_down)
    to_sibling(shared_at(0, x + 1, core), 6)
    send(own_direct, direct_at(x, core), x_send.at[0], x_recv.at[0], x_up)
    send(own_direct, direct_at(x, core), x_send.at[1], x_recv.at[1], x_down)
    own_along(1)
    hop(0, y + 2, 3, 7)
    across_along(1)
    send(hidden_ref.at[:, theirs], rows.at[pl.ds(0, count)], h_send.at[0], h_recv.at[0], partner)

    def heard(i, _):
        @pl.when(i != me)
        def _():
            landing(prompts.at[0, i], p_recv.at[0, i])

        landing(prompts.at[1, i], p_recv.at[1, i])
        landing(prompts.at[2, i], p_recv.at[2, i])
        return 0

    def give(half):
        def step(turn, _):
            i = ((2 + 3 * (turn // 2)) % 4) * 2 + turn % 2
            to_x, to_core = (x + i // 2) % 4, (core + i % 2) % 2
            at = to_x * 2 + to_core
            for kind in (1, 2, 0):
                low, size = SPANS[kind][half]
                span = pl.ds(low, size)
                outgoing[min(kind, 1), i, span] = states[half][
                    prompt_words[kind, at, 0, 0], pl.ds(low - HALVES[half][0], size)
                ]
                src = outgoing.at[min(kind, 1), i, span]
                dst = arrived_ref.at[fsdp, span]
                copy = remote(
                    src, dst, o_send.at[half, kind, i], o_recv.at[half, kind, me],
                    device(to_x, y + (0, 1, 3)[kind], z, to_core),
                )
                if kind == 0:
                    pl.when(i > 0)(copy.start)

                    @pl.when(i == 0)
                    def _():
                        pltpu.make_async_copy(src, dst, local_sem.at[9 + half]).start()
                else:
                    copy.start()
            return 0

        lax.fori_loop(0, 8, step, 0)

    lax.fori_loop(0, 8, heard, 0)
    local(prompts, prompt_words, 11).wait()
    far_states(0)
    give(0)
    hop(1, y, 1, 5)
    along_z(0)
    along_z(1)
    landing(shared_at(0, x + 2, core, 0, 256), w_recv.at[2])
    landing(shared_at(0, x + 2, core, 256, 256), w_recv.at[3])
    to_sibling(shared_at(0, x + 2, core), 7)
    hop(1, y + 2, 3, 7)
    landing(direct_at(x + 3, core), x_recv.at[0])
    first = direct_at(x + 3, core, 0, 256)
    send(first, first, x_send.at[2], x_recv.at[2], x_up)
    to_sibling(direct_at(x + 3, core), 8)
    landing(direct_at(x + 1, core), x_recv.at[1])
    second = direct_at(x + 1, core, 256, 256)
    send(second, second, x_send.at[3], x_recv.at[3], x_down)
    to_sibling(direct_at(x + 1, core), 9)
    lax.fori_loop(3, 6, prepare, 0)
    along_z(2)
    far_states(1)
    give(1)

    def multiply(weights_of, mine_to, theirs_to, theirs_in, slot):
        theirs_to[...] = dot_nn(rows[:count, :], weights_of[...])
        send(theirs_to, theirs_in, t_send.at[slot], t_recv.at[slot], partner)
        mine_to[...] = dot_nn(rows[count:, :], weights_of[...])

    def multiply_shared(step, slots):
        keep[step].wait()
        landing(shared_at(step, x, core + 1), d_recv.at[step])
        for dx, slot in zip(FAR, slots):
            landing(shared_at(step, x + dx, core + 1), d_recv.at[slot])
        multiply(shared.at[(z + step) % 4], total.at[step], partial.at[step], landed.at[step], step)

    landing(rows.at[pl.ds(0, count)], h_recv.at[0])
    keep_rows.wait()
    multiply_shared(0, (5, 6, 7))
    landing(direct_at(x + 2, core, 0, 256), x_recv.at[2])
    landing(direct_at(x + 2, core, 256, 256), x_recv.at[3])
    to_sibling(direct_at(x + 2, core), 10)
    lax.fori_loop(6, 8, prepare, 0)

    for at, dx in enumerate(FAR):
        landing(shared_at(3, x + dx, core), z_recv.at[at])
        first = shared_at(3, x + dx, core, 0, 256)
        send(first, first, z_send.at[6 + at], z_recv.at[6 + at], z_up)
        to_sibling(shared_at(3, x + dx, core), 11 + at)
        landing(shared_at(1, x + dx, core), z_recv.at[3 + at])
        second = shared_at(1, x + dx, core, 256, 256)
        send(second, second, z_send.at[9 + at], z_recv.at[9 + at], z_down)
        to_sibling(shared_at(1, x + dx, core), 14 + at)
        if at == 0:
            keep_direct.wait()
            landing(direct_at(x, core + 1), d_recv.at[4])
            for more, slot in zip(FAR, (8, 9, 10)):
                landing(direct_at(x + more, core + 1), d_recv.at[slot])
            multiply(direct, total_d, partial_d, landed_d, 4)
            lax.fori_loop(8, 11, prepare, 0)
        if at == 1:
            lax.fori_loop(11, 16, prepare, 0)
            leave = [local(inner, high_ref, 12), local(gate, low_ref, 13), local(gate_out, gate_out_ref, 14)]
    multiply_shared(3, (11, 12, 13))
    multiply_shared(1, (14, 15, 16))
    def last_part(xx, start, finish):
        deep = pl.ds(pl.multiple_of((xx % 4) * 1024, 1024), 1024)
        piece = shared[(z + 2) % 4, deep]
        theirs_now = dot_nn(rows[:count, deep], piece)
        partial[2] = theirs_now if start else partial[2] + theirs_now
        if finish:
            send(partial.at[2], landed.at[2], t_send.at[2], t_recv.at[2], partner)
        own_now = dot_nn(rows[count:, deep], piece)
        total[2] = own_now if start else total[2] + own_now

    def last_lands(at):
        here = x + FAR[at]
        landing(shared_at(2, here, core, 0, 256), z_recv.at[6 + at])
        landing(shared_at(2, here, core, 256, 256), z_recv.at[9 + at])
        to_sibling(shared_at(2, here, core), 17 + at)

    keep[2].wait()
    landing(shared_at(2, x, core + 1), d_recv.at[2])
    last_part(x, True, False)
    last_lands(0)
    last_lands(1)
    landing(shared_at(2, x + FAR[0], core + 1), d_recv.at[17])
    last_part(x + FAR[0], False, False)
    last_lands(2)
    landing(shared_at(2, x + FAR[1], core + 1), d_recv.at[18])
    last_part(x + FAR[1], False, False)
    landing(shared_at(2, x + FAR[2], core + 1), d_recv.at[19])
    last_part(x + FAR[2], False, True)

    landing(landed_d, t_recv.at[4])
    projected_ref[:, :DIRECT] = total_d[...] + landed_d[...]
    for step in (0, 3, 1, 2):
        landing(landed.at[step], t_recv.at[step])
        cols = pl.ds(pl.multiple_of(DIRECT + ((z + step) % 4) * SHARED, 128), SHARED)
        projected_ref[:, cols] = total[step] + landed[step]

    def settle(i, _):
        for half in range(2):
            @pl.when(i != me)
            def _():
                landing(arrived_ref.at[parity * 8 + i, pl.ds(*SPANS[0][half])], o_recv.at[half, 0, i])

            for kind in (1, 2):
                landing(arrived_ref.at[(1 - parity) * 8 + i, pl.ds(*SPANS[kind][half])], o_recv.at[half, kind, i])
            for kind in range(3):
                src = outgoing.at[min(kind, 1), i, pl.ds(*SPANS[kind][half])]
                copy = remote(src, src, o_send.at[half, kind, i], o_recv.at[half, kind, i], sibling)
                if kind == 0:
                    pl.when(i > 0)(copy.wait_send)
                else:
                    copy.wait_send()
        for kind in range(3):
            copy = remote(mine, mine, p_send.at[kind, i], p_recv.at[kind, i], sibling)
            if kind == 0:
                pl.when(i > 0)(copy.wait_send)
            else:
                copy.wait_send()
        return 0

    lax.fori_loop(0, 8, settle, 0)
    for half in range(2):
        span = pl.ds(*HALVES[half])
        pltpu.make_async_copy(outgoing.at[0, 0, span], arrived_ref.at[fsdp, span], local_sem.at[9 + half]).wait()
    for copy in leave:
        copy.wait()
    for copy in sent:
        copy.wait_send()


def exchange(
    hidden, weight, states, conv_state, prompt, inner_raw, gate_raw, step_raw, decay_log, step_bias, conv_weight, conv_bias
):
    count, features = inner_raw.shape
    columns = weight.shape[1]
    heads = step_raw.shape[1]
    deep = PIECE + EXTRA
    dma = lambda *shape: pltpu.SemaphoreType.DMA(shape)
    anywhere = pl.BlockSpec(memory_space=pl.ANY)
    inside = pl.BlockSpec(memory_space=pltpu.VMEM)
    return pl.pallas_call(
        exchange_kernel,
        in_specs=[pl.BlockSpec(memory_space=pltpu.SMEM)] + [anywhere] * 5 + [inside] * 6,
        out_specs=[inside, anywhere, anywhere, anywhere, anywhere, inside],
        out_shape=[
            jax.ShapeDtypeStruct((count, columns), F32),
            jax.ShapeDtypeStruct((16, deep, 256), BF16),
            jax.ShapeDtypeStruct((count, features), BF16),
            jax.ShapeDtypeStruct((count, features), BF16),
            jax.ShapeDtypeStruct((count, features), F32),
            jax.ShapeDtypeStruct((HEAD_ROWS, features), F32),
        ],
        scratch_shapes=[
            pltpu.VMEM((4, 4096, SHARED), BF16),
            pltpu.VMEM((4096, DIRECT), BF16),
            pltpu.VMEM((2 * count, 4096), BF16),
            pltpu.VMEM((16, HALVES[0][1], 256), BF16),
            pltpu.VMEM((16, HALVES[1][1], 256), BF16),
            pltpu.VMEM((2, 8, deep, 256), BF16),
            pltpu.VMEM((3, 8, 8, 128), jnp.int32),
            pltpu.SMEM((3, 8, 8, 128), jnp.int32),
            pltpu.VMEM((4, count, SHARED), F32),
            pltpu.VMEM((4, count, SHARED), F32),
            pltpu.VMEM((4, count, SHARED), F32),
            pltpu.VMEM((count, DIRECT), F32),
            pltpu.VMEM((count, DIRECT), F32),
            pltpu.VMEM((count, DIRECT), F32),
            pltpu.VMEM((count, features), BF16),
            pltpu.VMEM((count, features), BF16),
            pltpu.VMEM((count, features), F32),
            pltpu.VMEM((count + 8, PIECE), F32),
            pltpu.VMEM((2 * heads, PIECE), jnp.int32),
            pltpu.VMEM((count, 2 * heads), BF16),
            pltpu.VMEM((count, 2 * heads), BF16),
            dma(4), dma(4), dma(4), dma(4), dma(12), dma(12), dma(20), dma(20), dma(2, 9), dma(2, 9),
            dma(2, 3, 8), dma(2, 3, 8), dma(3, 8), dma(3, 8), dma(1), dma(1), dma(5), dma(5), dma(16),
        ],
        compiler_params=pltpu.CompilerParams(
            collective_id=0, has_side_effects=True, vmem_limit_bytes=62 * 2**20
        ),
        cost_estimate=pl.CostEstimate(flops=9 * 10**9, bytes_accessed=2**25, transcendentals=0),
        name="exchange",
    )(
        prompt, hidden, weight, states, inner_raw, gate_raw, step_raw, decay_log, step_bias, conv_weight,
        conv_bias, conv_state.transpose(1, 0, 2),
    )


def on_device(
    hidden, inner_raw, gate_raw, step_raw, proj_weight, conv_weight, conv_bias, decay_log, step_bias,
    norm_gain, ssm_state, conv_state, slot_prompt, slot_len,
):
    conv_bias = conv_bias[None, :]
    own_states = ssm_state.reshape(ssm_state.shape[0], PIECE, ssm_state.shape[3])
    projected, state, high, low, gate, factor = exchange(
        hidden, proj_weight, own_states, conv_state, slot_prompt, inner_raw, gate_raw, step_raw, decay_log[None, :],
        step_bias[None, :], conv_weight, conv_bias,
    )
    return after(
        slot_len, projected, conv_weight, conv_bias, state, inner_raw, factor, high, low, gate,
        norm_gain[None, :],
    )


def solution(mesh):
    rows = P(("dp", "fsdp"), None)
    in_specs = (
        rows, rows, rows, rows, P("fsdp", None), P(), P(), P(), P(), P(),
        P("dp", "fsdp", None, None), P("dp", None, None), P(("dp", "fsdp")), P(("dp", "fsdp")),
    )
    return jax.shard_map(on_device, mesh=mesh, in_specs=in_specs, out_specs=rows, check_vma=False)
```
